256 devices in a mesh: seq: 64 (over y, z, core), dp: 4 (over x).
Axes of the slice: x: 4, y: 4, z: 8, core: 2. Of those that a mesh axis runs over, the one named last changes fastest.
Arguments:
- inputs: bfloat16 [4, 16384, 1024], P('dp', 'seq'), may hold values from -24 to 24
- gates: bfloat16 [4, 16384, 1024], P('dp', 'seq'), may hold values from -6 to 6
- pairs: bfloat16 [4, 16384, 128], P('dp', 'seq'), may hold values from -2.09375 to 2.09375
- steps: float32 [4, 16, 16384], P('dp', None, 'seq'), may hold values from 0.004 to 0.1
- log_decay: float32 [16], replicated, may hold values from -12 to 1
- skip: float32 [16], replicated, may hold values from 0.5 to 1.5
- gain: float32 [1024], replicated, may hold values from 0.1 to 1.9
- out_weight: bfloat16 [1024, 1024], replicated, may hold values from -0.1875 to 0.1875
- out_grad: bfloat16 [4, 16384, 1024], P('dp', 'seq'), may hold values from -40 to 40
- order_ids: int32 [2], replicated, may hold values from 0 to 3
Outputs:
- input_grad: bfloat16 [4, 16384, 1024], P('dp', 'seq')
- gate_grad: bfloat16 [4, 16384, 1024], P('dp', 'seq')
- pair_grad: bfloat16 [4, 16384, 128], P('dp', 'seq')
- weight_grad: float32 [1024, 1024], replicated
- gain_grad: float32 [1024], replicated
- skip_grad: float32 [16], replicated
The draws below stay inside these ranges and needn't reach their ends.
Inputs may be any that keep to these rules, and one draw needn't show every extreme that they name: order_ids[0] picks this layer's row order and order_ids[1] the next layer's column order.
All inputs are finite; a program needn't handle non-finite values.
Results may differ from the reference program's by a relative error of at most 0.0039.
Values may be sent and summed in bfloat16 or wider, within the bound.
A program may use at most 128 MiB of HBM per device.

```python
import math
import jax
import jax.numpy as jnp
from jax import lax

D = 1024
HEADS = 16
HEAD_DIM = 64
STATE = 64
INNER = 1024
IMG_W = 256
TOKENS = 16384
IMG_H = 64
IMAGES = 4
BLOCK = 128


def draw_inputs(key, part):
    key = jax.random.fold_in(key, 11)
    first, second, third = jax.random.split(key, 3)
    shape = (IMAGES, TOKENS, HEADS * HEAD_DIM)
    rows = jnp.exp(jax.random.uniform(second, (IMAGES, TOKENS, 1), minval=math.log(0.3), maxval=math.log(3.0)))
    columns = jnp.exp(jax.random.uniform(third, (1, 1, shape[2]), minval=math.log(0.6), maxval=math.log(1.7)))
    base = jnp.clip(jax.random.normal(first, shape), -4.0, 4.0)
    return (base * rows * columns).astype(jnp.bfloat16)


def draw_steps(key, part):
    key = jax.random.fold_in(key, 31)
    first, second = jax.random.split(key)
    count = TOKENS // BLOCK
    rough = jnp.exp(jax.random.uniform(first, (IMAGES, HEADS, count, BLOCK), minval=math.log(0.01), maxval=math.log(0.05)))
    factor = jnp.exp(jax.random.uniform(second, (IMAGES, HEADS, count, 1), minval=math.log(0.5), maxval=math.log(2.0)))
    return (rough * factor).reshape(IMAGES, HEADS, TOKENS).astype(jnp.float32)


def draw_log_decay(key, part):
    key = jax.random.fold_in(key, 23)
    first, second, third = jax.random.split(key, 3)
    fast_share = 0.5
    fast = jax.random.uniform(first, (HEADS,)) < fast_share
    fast_rate = jnp.exp(jax.random.uniform(second, (HEADS,), minval=math.log(0.7), maxval=math.log(1.4)))
    slow_total = jnp.exp(jax.random.uniform(third, (HEADS,), minval=math.log(0.3), maxval=math.log(1.5)))
    slow_rate = slow_total / (0.025 * TOKENS)
    return jnp.log(jnp.where(fast, fast_rate, slow_rate)).astype(jnp.float32)


def draw_out_grad(key, part):
    key = jax.random.fold_in(key, 47)
    first, second = jax.random.split(key)
    shape = (IMAGES, TOKENS, D)
    rise = jnp.exp(math.log(3.0) * jnp.arange(TOKENS, dtype=jnp.float32) / TOKENS)[None, :, None]
    rows = jnp.exp(jax.random.uniform(second, (IMAGES, TOKENS, 1), minval=math.log(0.5), maxval=math.log(2.0)))
    base = jnp.clip(jax.random.normal(first, shape), -4.0, 4.0)
    return (base * rise * rows).astype(jnp.bfloat16)


def steps_of(stream_key, shape, cuts, least, high):
    def one(dim, parts):
        steps = jax.random.uniform(jax.random.fold_in(jax.random.fold_in(stream_key, 6), dim), (parts,), jnp.float32, least / len(cuts), high / len(cuts))
        return jnp.repeat(jnp.exp(steps), shape[dim] // parts).reshape((-1,) + (1,) * (len(shape) - dim - 1))

    level = one(*cuts[0])
    for cut in cuts[1:]:
        level = level * one(*cut)
    return level


def gaussian(rng, dims, spread, most, shards=(), kind=jnp.bfloat16):
    drawn = spread * jax.random.normal(rng, dims, jnp.float32)
    if shards:
        drawn = drawn * steps_of(rng, dims, shards, -0.22, 0.18)
    return jnp.clip(drawn, -most, most).astype(kind)


def setup_inputs(seed: int = 0) -> dict:
    streams_of = jax.random.split(jax.random.key(seed), 11)
    inputs = draw_inputs(jax.random.fold_in(streams_of[10], 71), 0)
    gates = gaussian(streams_of[1], (IMAGES, TOKENS, INNER), 1.5, 6.0, ((0, 4), (1, 64)))
    pairs = gaussian(streams_of[2], (IMAGES, TOKENS, 2 * STATE), 0.35, 2.09375, ((0, 4), (1, 64)))
    steps = draw_steps(jax.random.fold_in(streams_of[10], 71), 0)
    log_decay = draw_log_decay(jax.random.fold_in(streams_of[10], 71), 0)
    skip = jnp.clip(jax.random.uniform(streams_of[5], (HEADS,), jnp.float32, 0.5, 1.5), 0.5, 1.5)
    gain = jnp.clip(1.0 + 0.18 * jax.random.normal(streams_of[6], (INNER,), jnp.float32), 0.1, 1.9)
    out_weight = gaussian(streams_of[7], (INNER, D), INNER ** -0.5, 0.1875)
    out_grad = draw_out_grad(jax.random.fold_in(streams_of[10], 71), 0)
    order_ids = jax.random.randint(streams_of[9], (2,), 0, 4).astype(jnp.int32)
    return dict(inputs=inputs, gates=gates, pairs=pairs, steps=steps, log_decay=log_decay, skip=skip, gain=gain, out_weight=out_weight, out_grad=out_grad, order_ids=order_ids)


HIGH_ACCURACY = lax.Precision.HIGHEST
EPSILON = 1e-05

def row_order_cells(order, position):
    line = position // IMG_W
    offset = position % IMG_W
    plain = jnp.where(line % 2 == 0, offset, IMG_W - 1 - offset)
    row = jnp.where(order % 2 == 1, IMG_H - 1 - line, line)
    column = jnp.where(order // 2 == 1, IMG_W - 1 - plain, plain)
    return (row, column)

def column_order_position(order, row, column):
    line = jnp.where(order // 2 == 1, IMG_W - 1 - column, column)
    across = jnp.where(order % 2 == 1, IMG_H - 1 - row, row)
    offset = jnp.where(line % 2 == 0, across, IMG_H - 1 - across)
    return (line * IMG_H + offset).astype(jnp.int32)

def state_space(value_rows, input_b_matrix, input_c_matrix, step_sizes, rates):
    count = TOKENS // BLOCK
    value_blocks = value_rows.reshape(count, BLOCK, HEADS, HEAD_DIM)
    b_blocks = input_b_matrix.reshape(count, BLOCK, STATE)
    c_blocks = input_c_matrix.reshape(count, BLOCK, STATE)
    step_size_blocks = step_sizes.reshape(HEADS, count, BLOCK).transpose(1, 0, 2)
    lower = jnp.tril(jnp.ones((BLOCK, BLOCK), dtype=bool))

    @jax.checkpoint
    def advance(carry, block):
        part_x, part_b, part_c, part_s = block
        logs = part_s * rates[:, None]
        cumul = jnp.cumsum(logs, axis=1)
        gaps = cumul[:, :, None] - cumul[:, None, :]
        weights = jnp.where(lower, jnp.exp(jnp.where(lower, gaps, 0.0)), 0.0)
        intersection = jnp.dot(part_c, part_b.T, precision=HIGH_ACCURACY)
        mixing = weights * intersection[None] * part_s[:, None, :]
        output = jnp.einsum('hij,jhp->ihp', mixing, part_x, precision=HIGH_ACCURACY)
        output = output + jnp.einsum('hi,hpn,in->ihp', jnp.exp(cumul), carry, part_c, precision=HIGH_ACCURACY)
        block_tail_states = jnp.exp(cumul[:, -1:] - cumul) * part_s
        fresh = jnp.einsum('hj,jhp,jn->hpn', block_tail_states, part_x, part_b, precision=HIGH_ACCURACY)
        carry = jnp.exp(cumul[:, -1])[:, None, None] * carry + fresh
        return (carry, output)
    start = jnp.zeros((HEADS, HEAD_DIM, STATE), jnp.float32)
    final, outputs = lax.scan(advance, start, (value_blocks, b_blocks, c_blocks, step_size_blocks))
    return outputs.reshape(TOKENS, HEADS, HEAD_DIM)

def reference(inputs, gates, pairs, steps, log_decay, skip, gain, out_weight, out_grad, order_ids):
    rates = -jnp.exp(log_decay)
    this_order = order_ids[0]
    next_order = order_ids[1]
    position = jnp.arange(TOKENS, dtype=jnp.int32)
    row, column = row_order_cells(this_order, position)
    source = column_order_position(next_order, row, column)

    def one_image(items):
        image_in, image_gate, image_pair, image_step, image_grad = items
        grads = jnp.take(image_grad, source, axis=0)
        value_rows = image_in.astype(jnp.float32).reshape(TOKENS, HEADS, HEAD_DIM)
        input_b_matrix = image_pair[:, :STATE].astype(jnp.float32)
        input_c_matrix = image_pair[:, STATE:].astype(jnp.float32)

        def core_fn(value_arg, b_arg, c_arg):
            return state_space(value_arg, b_arg, c_arg, image_step, rates)
        core, pullback = jax.vjp(core_fn, value_rows, input_b_matrix, input_c_matrix)
        mixed = (core + skip[None, :, None] * value_rows).reshape(TOKENS, INNER)
        gate_f = image_gate.astype(jnp.float32)
        sigma = jax.nn.sigmoid(gate_f)
        active = gate_f * sigma
        gated = mixed * active
        inverse = lax.rsqrt(lax.optimization_barrier(jnp.mean(gated * gated, axis=1, keepdims=True)) + EPSILON)
        unit = gated * inverse
        normed = (unit * gain).astype(jnp.bfloat16)
        weight_part = jnp.dot(normed.T, grads, preferred_element_type=jnp.float32)
        d_normed = jnp.dot(grads, out_weight.T, preferred_element_type=jnp.float32)
        scaled = d_normed * gain
        d_gated = inverse * (scaled - unit * lax.optimization_barrier(jnp.mean(scaled * unit, axis=1, keepdims=True)))
        gain_part = lax.optimization_barrier(jnp.sum(d_normed * unit, axis=0))
        gate_part = (d_gated * mixed * sigma * (1.0 + gate_f * (1.0 - sigma))).astype(jnp.bfloat16)
        d_mixed = (d_gated * active).reshape(TOKENS, HEADS, HEAD_DIM)
        skip_part = lax.optimization_barrier(jnp.sum(d_mixed * value_rows, axis=(0, 2)))
        d_core, b_matrix_gradient, c_matrix_gradient = pullback(d_mixed)
        input_part = (d_core + skip[None, :, None] * d_mixed).reshape(TOKENS, INNER).astype(jnp.bfloat16)
        pair_part = jnp.concatenate([b_matrix_gradient, c_matrix_gradient], axis=1).astype(jnp.bfloat16)
        return (input_part, gate_part, pair_part, weight_part, gain_part, skip_part)
    results = lax.map(one_image, (inputs, gates, pairs, steps, out_grad))
    input_grad, gate_grad, pair_grad, weight_parts, gain_parts, skip_parts = results
    return (input_grad, gate_grad, pair_grad, lax.optimization_barrier(jnp.sum(weight_parts, axis=0)), lax.optimization_barrier(jnp.sum(gain_parts, axis=0)), lax.optimization_barrier(jnp.sum(skip_parts, axis=0)))
```

```python
import functools

import jax
import jax.numpy as jnp
from jax import lax
from jax.experimental import pallas as pl
from jax.experimental.pallas import tpu as pltpu
from jax.sharding import PartitionSpec as P

F32 = jnp.float32
BF16 = jnp.bfloat16
MESH = pl.DeviceIdType.MESH
EPSILON = 1e-05
T = 256
W = 1024
HEADS = 16
STATE = 64
SEQ, NX, NY, NZ, GROUP = 64, 4, 4, 8, 16
VMEM_LIMIT = 56 * 1024 * 1024


def iota(shape, dim):
    return lax.broadcasted_iota(jnp.int32, shape, dim)


def mm(a, b, ca=1, cb=0):
    return lax.dot_general(a, b, (((ca,), (cb,)), ((), ())), preferred_element_type=F32)


def split(a):
    high = a.astype(BF16)
    return high, (a - high.astype(F32)).astype(BF16)


def mm_exact_left(a, b, ca=1, cb=0):
    high, low = split(b)
    return mm(a, high, ca, cb) + mm(a, low, ca, cb)


def mm_exact_right(a, b, ca=1, cb=0):
    high, low = split(a)
    return mm(high, b, ca, cb) + mm(low, b, ca, cb)


def mm_split(a, b, ca=1, cb=0):
    ah, al = split(a)
    bh, bl = split(b)
    return mm(ah, bh, ca, cb) + (mm(ah, bl, ca, cb) + mm(al, bh, ca, cb))


def expand(small):
    spread = (iota((HEADS, W), 1) // (W // HEADS) == iota((HEADS, W), 0)).astype(F32).astype(BF16)
    high = small.astype(BF16)
    rest = small - high.astype(F32)
    mid = rest.astype(BF16)
    low = (rest - mid.astype(F32)).astype(BF16)
    return mm(high, spread) + (mm(mid, spread) + mm(low, spread))


def scales(steps, log_decay):
    token_steps = steps.T
    lower = (iota((T, T), 0) >= iota((T, T), 1)).astype(F32)
    logs = lax.dot_general(
        lower,
        token_steps * (-jnp.exp(log_decay)),
        (((1,), (0,)), ((), ())),
        precision=lax.Precision.HIGHEST,
        preferred_element_type=F32,
    )
    mid = 0.5 * logs[T - 1 : T, :]
    up = expand(jnp.exp(logs - mid))
    down = expand(jnp.exp(mid - logs) * token_steps)
    half = expand(jnp.broadcast_to(jnp.exp(mid), (8, HEADS)))
    return up, down, half


def place():
    s = lax.axis_index("seq")
    return s, lax.axis_index("dp"), s // GROUP, s % GROUP


def copy_to(src, dst, send, recv, seq, dp):
    return pltpu.make_async_remote_copy(
        src_ref=src, dst_ref=dst, send_sem=send, recv_sem=recv, device_id={"seq": seq, "dp": dp}, device_id_type=MESH
    )


class StateExchange:
    SCRATCH = [
        pltpu.VMEM((GROUP, 5, 8, 128), F32),
        pltpu.VMEM((GROUP, 5, 8, 128), F32),
        pltpu.VMEM((5, 8, 128), F32),
        pltpu.VMEM((NY, 5, 8, 128), F32),
        pltpu.VMEM((GROUP, 4, 8, 128), F32),
        pltpu.VMEM((GROUP, 4, 8, 128), F32),
        pltpu.SemaphoreType.DMA((GROUP,)),
        pltpu.SemaphoreType.DMA((GROUP,)),
        pltpu.SemaphoreType.DMA((NY,)),
        pltpu.SemaphoreType.DMA((NY,)),
        pltpu.SemaphoreType.DMA((GROUP,)),
        pltpu.SemaphoreType.DMA((GROUP,)),
    ]

    def __init__(self, refs, reverse):
        self.out, self.inc, self.tot, self.tots, self.ans, self.got = refs[:6]
        self.s1, self.r1, self.s2, self.r2, self.s3, self.r3 = refs[6:]
        self.reverse = reverse
        self.s, self.x, self.y, self.m = place()

    def first(self, i):
        to = (self.m + i) % GROUP
        return copy_to(
            self.out.at[to], self.inc.at[self.m], self.s1.at[i], self.r1.at[i], self.y * GROUP + to, self.x
        )

    def second(self, i):
        to = (self.y + i) % NY
        return copy_to(self.tot, self.tots.at[self.y], self.s2.at[i], self.r2.at[i], to * GROUP + self.m, self.x)

    def third(self, i):
        to = (self.m + i) % GROUP
        return copy_to(
            self.ans.at[to], self.got.at[self.m], self.s3.at[i], self.r3.at[i], self.y * GROUP + to, self.x
        )

    @staticmethod
    def each(count, act):
        def body(i, carry):
            act(i)
            return carry

        lax.fori_loop(1, count, body, 0)

    def fill(self, state, decay):
        for b in range(8):
            lanes = slice(128 * b, 128 * b + 128)
            for k in range(4):
                self.out[:, k, b, :] = state[GROUP * k : GROUP * k + GROUP, lanes]
            self.out[:, 4, b, :] = jnp.broadcast_to(decay[0:1, lanes], (GROUP, 128))

    def start(self):
        self.each(GROUP, lambda i: self.first(i).start())
        self.inc[pl.ds(self.m, 1)] = self.out[pl.ds(self.m, 1)]

    def fold(self):
        self.each(GROUP, lambda i: self.first(i).wait())

        def body(i, carry):
            total, decay = carry
            j = GROUP - 1 - i if self.reverse else i
            block = self.inc[pl.ds(j, 1)][0]
            self.inc[pl.ds(j, 1), 0:4] = total[None]
            self.inc[pl.ds(j, 1), 4:5] = decay[None, None]
            factor = block[4]
            return factor[None] * total + block[0:4], factor * decay

        total, decay = lax.fori_loop(0, GROUP, body, (jnp.zeros((4, 8, 128), F32), jnp.ones((8, 128), F32)))
        self.tot[0:4] = total
        self.tot[4:5] = decay[None]
        self.each(NY, lambda i: self.second(i).start())
        self.tots[pl.ds(self.y, 1), 0:4] = total[None]
        self.tots[pl.ds(self.y, 1), 4:5] = decay[None, None]

    def answer(self):
        self.each(NY, lambda i: self.second(i).wait())
        before = jnp.zeros((4, 8, 128), F32)
        for k in range(NY):
            j = NY - 1 - k if self.reverse else k
            reached = (self.y < j) if self.reverse else (self.y > j)
            block = self.tots[j]
            flag = jnp.full((4, 8, 128), reached.astype(jnp.int32)) > 0
            before = jnp.where(flag, block[4][None] * before + block[0:4], before)

        def body(j, carry):
            block = self.inc[pl.ds(j, 1)][0]
            self.ans[pl.ds(j, 1)] = (block[0:4] + block[4][None] * before)[None]
            return carry

        lax.fori_loop(0, GROUP, body, 0)
        self.each(GROUP, lambda i: self.third(i).start())
        self.got[pl.ds(self.m, 1)] = self.ans[pl.ds(self.m, 1)]

    def finish(self, state_ref):
        self.each(GROUP, lambda i: self.third(i).wait())
        for b in range(8):
            for k in range(4):
                state_ref[GROUP * k : GROUP * k + GROUP, 128 * b : 128 * b + 128] = self.got[:, k, b, :]


NSTATE = len(StateExchange.SCRATCH)


def forward_kernel(orders, og_ref, x_ref, pairs_ref, steps_ref, decay_ref, grads_ref, state_ref, out, inc, ssem, rsem, *refs):
    s, x, _, _ = place()
    barrier = pltpu.get_barrier_semaphore()

    def greet(i, carry):
        pl.semaphore_signal(barrier, inc=1, device_id={"seq": (s + i) % SEQ, "dp": x}, device_id_type=MESH)
        return carry

    lax.fori_loop(1, SEQ, greet, 0)

    states = StateExchange(refs, False)
    _, down, half = scales(steps_ref[...], decay_ref[...])
    fresh = mm_exact_left(pairs_ref[:, 0:STATE], down * x_ref[...].astype(F32), 0, 0)
    states.fill(half[0:1] * fresh, half * half)

    flip_rows = (orders[0] + orders[1]) % 2
    flip_columns = (orders[0] // 2 + orders[1] // 2 + s) % 2
    row = iota((4 * T, T), 0)
    device, quarter, line = row // 16, (row // 4) % 4, row % 4
    token = line * SEQ + jnp.where((line + flip_rows) % 2 == 0, device, SEQ - 1 - device)
    column = iota((4 * T, T), 1)
    packed = jnp.zeros((4 * T, T), F32)
    for j in range(4):
        pick = jnp.where((token == column) & (quarter == j), 1.0, 0.0).astype(BF16)
        packed = packed + mm(pick, og_ref[:, 256 * j : 256 * j + 256])
    out[...] = packed.astype(BF16).reshape(SEQ, 16, 256)

    pl.semaphore_wait(barrier, SEQ - 1)
    states.start()

    def swap(i):
        to = (s + i) % SEQ
        return copy_to(out.at[to], inc.at[s], ssem.at[i], rsem.at[i], to, x)

    StateExchange.each(SEQ, lambda i: swap(i).start())
    inc[pl.ds(s, 1)] = out[pl.ds(s, 1)]
    states.fold()
    states.answer()
    states.finish(state_ref)
    StateExchange.each(SEQ, lambda i: swap(i).wait())

    arrived = inc[...].reshape(4 * T, 256)
    place_ = iota((T, 4 * T), 0)
    source = jnp.where(flip_columns == 0, place_, T - 1 - place_)
    source = (source // 4) * 16 + source % 4
    column = iota((T, 4 * T), 1)
    for j in range(4):
        pick = jnp.where(source + 4 * j == column, 1.0, 0.0).astype(BF16)
        grads_ref[:, 256 * j : 256 * j + 256] = mm(pick, arrived).astype(BF16)


def middle_kernel(
    x_ref, z_ref, pairs_ref, steps_ref, decay_ref, skip_ref, gain_ref, weight_ref, grads_ref, state_ref,
    gate_grad_ref, normed_ref, d_mixed_ref, returns_ref, sums_ref,
):
    up, down, half = scales(steps_ref[...], decay_ref[...])
    x = x_ref[...].astype(F32)
    b, c = pairs_ref[:, 0:STATE], pairs_ref[:, STATE : 2 * STATE]
    lower = iota((T, T), 0) >= iota((T, T), 1)
    mixing = jnp.where(lower, mm(c, b, 1, 1), 0.0)
    inner = mm_split(mixing, down * x) + mm_exact_left(c, half[0:1] * state_ref[...])
    skip = expand(jnp.broadcast_to(skip_ref[...], (8, HEADS)))[0:1]
    mixed = up * inner + skip * x
    gate = z_ref[...].astype(F32)
    sigma = jax.nn.sigmoid(gate)
    active = gate * sigma
    gated = mixed * active
    inverse = lax.rsqrt(jnp.mean(gated * gated, axis=1, keepdims=True) + EPSILON)
    unit = gated * inverse
    gain = gain_ref[...]
    normed_ref[...] = (unit * gain).astype(BF16)
    d_normed = mm(grads_ref[...], weight_ref[...], 1, 1)
    scaled = d_normed * gain
    d_gated = inverse * (scaled - unit * jnp.mean(scaled * unit, axis=1, keepdims=True))
    gate_grad_ref[...] = (d_gated * mixed * sigma * (1.0 + gate * (1.0 - sigma))).astype(BF16)
    d_mixed = d_gated * active
    d_mixed_ref[...] = d_mixed
    sums_ref[0:1] = jnp.sum(d_normed * unit, axis=0, keepdims=True)
    sums_ref[1:2] = jnp.sum(d_mixed * x, axis=0, keepdims=True)
    returns_ref[...] = half[0:1] * mm_exact_left(c, up * d_mixed, 0, 0)


def backward_kernel(
    normed_ref, grads_ref, returns_ref, steps_ref, decay_ref, sums_ref,
    full, leaving_ref, total_ref,
    peer_normed, peer_grads, mine, rough, a1, b1, ra1, rb1, ra2, rb2, c1, r3, g3,
    t0, t1, t2, t3, tr0, tr1, tr2, tr3,
    s0, q0, sa, qa, sb, qb, sa2, qa2, sb2, qb2, s3, q3, s4, q4, sa5, qa5, sb5, qb5, sa6, qa6, sb6, qb6, s7, q7,
    ts0, tq0, ts1, tq1, ts2, tq2, ts3, tq3,
    *refs,
):
    s, x, y, m = place()
    z, core = m // 2, m % 2
    other = s + 1 - 2 * core
    barrier = pltpu.get_barrier_semaphore()

    def hello(seq, dp):
        pl.semaphore_signal(barrier, inc=1, device_id={"seq": seq, "dp": dp}, device_id_type=MESH)

    StateExchange.each(GROUP, lambda i: hello(y * GROUP + (m + i) % GROUP, x))
    StateExchange.each(NY, lambda i: hello(((y + i) % NY) * GROUP + m, x))
    StateExchange.each(NX, lambda i: hello(s, (x + i) % NX))

    states = StateExchange(refs, True)
    _, _, half = scales(steps_ref[...], decay_ref[...])
    states.fill(returns_ref[...], half * half)
    t0[...] = jnp.zeros_like(t0)
    t0[0:2] = sums_ref[...]
    pl.semaphore_wait(barrier, GROUP - 1 + NY - 1 + NX - 1)

    def along_x(i):
        return s, (x + i) % NX

    def along_y(i):
        return ((y + i) % NY) * GROUP + m, x

    def along_z(i):
        return y * GROUP + ((z + i) % NZ) * 2 + core, x

    def sum_round(count, out, inc, ss, rr, peer):
        return [copy_to(out, inc.at[i - 1], ss.at[i], rr.at[i], *peer(i)) for i in range(1, count)]

    def begin(copies):
        for one in copies:
            one.start()

    def end(copies):
        for one in copies:
            one.wait()

    pair = [
        copy_to(grads_ref, peer_grads, s0.at[0], q0.at[0], other, x),
        copy_to(
            normed_ref.at[:, pl.ds(pl.multiple_of((1 - core) * 512, 512), 512)],
            peer_normed, s0.at[1], q0.at[1], other, x,
        ),
        copy_to(t0, tr0, ts0.at[0], tq0.at[0], other, x),
    ]
    begin(pair)
    states.start()
    own = normed_ref[:, pl.ds(pl.multiple_of(core * 512, 512), 512)]
    mine[...] = mm(own, grads_ref[...], 0, 0)
    end(pair)
    mine[...] += mm(peer_normed[...], peer_grads[...], 0, 0)
    rough[...] = mine[...].astype(BF16)
    t1[...] = t0[...] + tr0[...]

    left, right = pl.ds(0, 512), pl.ds(512, 512)

    def rows(i, size, base=0):
        return pl.ds(pl.multiple_of(base + i * size, size), size)

    first = []
    for i in range(1, NX):
        first.append(copy_to(rough.at[rows((x + i) % NX, 128), left], ra1.at[i - 1], sa.at[i], qa.at[i], *along_x(i)))
        first.append(copy_to(rough.at[rows((y + i) % NY, 128), right], rb1.at[i - 1], sb.at[i], qb.at[i], *along_y(i)))
    first += sum_round(NX, t1, tr1, ts1, tq1, along_x)
    begin(first)
    states.fold()
    end(first)
    a1[...] = mine[rows(x, 128), 0:512] + (ra1[0].astype(F32) + ra1[1].astype(F32) + ra1[2].astype(F32))
    b1[...] = mine[rows(y, 128), 512:1024] + (rb1[0].astype(F32) + rb1[1].astype(F32) + rb1[2].astype(F32))
    t2[...] = t1[...] + tr1[0] + tr1[1] + tr1[2]
    second = []
    for i in range(1, NY):
        second.append(copy_to(a1.at[rows((y + i) % NY, 32)], ra2.at[i - 1], sa2.at[i], qa2.at[i], *along_y(i)))
        second.append(copy_to(b1.at[rows((x + i) % NX, 32)], rb2.at[i - 1], sb2.at[i], qb2.at[i], *along_x(i)))
    second += sum_round(NY, t2, tr2, ts2, tq2, along_y)
    begin(second)
    states.answer()
    end(second)
    a2 = a1[rows(y, 32), :] + ra2[0] + ra2[1] + ra2[2]
    b2 = b1[rows(x, 32), :] + rb2[0] + rb2[1] + rb2[2]
    t3[...] = t2[...] + tr2[0] + tr2[1] + tr2[2]
    for k in range(4):
        part = (slice(16 * (k // 2), 16 * (k // 2) + 16), slice(256 * (k % 2), 256 * (k % 2) + 256))
        c1[k] = a2[part]
        c1[k + 4] = b2[part]
    third = [
        copy_to(c1.at[(z + i) % NZ], r3.at[i - 1], s3.at[i], q3.at[i], *along_z(i)) for i in range(1, NZ)
    ] + sum_round(NZ, t3, tr3, ts3, tq3, along_z)
    begin(third)
    states.finish(leaving_ref)
    end(third)
    block = c1[pl.ds(z, 1)][0]
    total = t3[...]
    for i in range(NZ - 1):
        block = block + r3[i]
        total = total + tr3[i]
    total_ref[...] = total[0:2]
    g3[pl.ds(z, 1)] = block.astype(BF16)[None]
    fourth = [
        copy_to(g3.at[z], g3.at[z], s4.at[i], q4.at[i], *along_z(i)) for i in range(1, NZ)
    ]
    begin(fourth)
    end(fourth)
    base = core * 512
    for k in range(4):
        lanes = slice(256 * (k % 2), 256 * (k % 2) + 256)
        full[rows(k // 2, 16, base + 128 * x + 32 * y), lanes] = g3[k]
        lanes = slice(512 + 256 * (k % 2), 512 + 256 * (k % 2) + 256)
        full[rows(k // 2, 16, base + 128 * y + 32 * x), lanes] = g3[k + 4]
    fifth = []
    at_a = full.at[rows(y, 32, base + 128 * x), left]
    at_b = full.at[rows(x, 32, base + 128 * y), right]
    for i in range(1, NX):
        fifth.append(copy_to(at_a, at_a, sa5.at[i], qa5.at[i], *along_y(i)))
        fifth.append(copy_to(at_b, at_b, sb5.at[i], qb5.at[i], *along_x(i)))
    begin(fifth)
    end(fifth)
    at_a = full.at[rows(x, 128, base), left]
    at_b = full.at[rows(y, 128, base), right]
    sixth = []
    for i in range(1, NX):
        sixth.append(copy_to(at_a, at_a, sa6.at[i], qa6.at[i], *along_x(i)))
        sixth.append(copy_to(at_b, at_b, sb6.at[i], qb6.at[i], *along_y(i)))
    begin(sixth)
    last = []

    def hand_over(at, k):
        one = copy_to(at, at, s7.at[k], q7.at[k], other, x)
        one.start()
        last.append(one)

    hand_over(at_a, 0)
    hand_over(at_b, 1)
    for i in range(1, NX):
        sixth[2 * i - 2].wait()
        hand_over(full.at[rows((x + NX - i) % NX, 128, base), left], 2 * i)
        sixth[2 * i - 1].wait()
        hand_over(full.at[rows((y + NY - i) % NY, 128, base), right], 2 * i + 1)
    end(last)


def final_kernel(
    x_ref, pairs_ref, steps_ref, decay_ref, skip_ref, d_mixed_ref, state_ref, leaving_ref, input_grad_ref, pair_grad_ref
):
    up, down, half = scales(steps_ref[...], decay_ref[...])
    b, c = pairs_ref[:, 0:STATE], pairs_ref[:, STATE : 2 * STATE]
    lower = iota((T, T), 0) >= iota((T, T), 1)
    mixing = jnp.where(lower, mm(c, b, 1, 1), 0.0)
    d_mixed = d_mixed_ref[...]
    pulled = up * d_mixed
    pushed = down * x_ref[...].astype(F32)
    entering = half[0:1] * state_ref[...]
    leaving = half[0:1] * leaving_ref[...]
    skip = expand(jnp.broadcast_to(skip_ref[...], (8, HEADS)))[0:1]
    d_x = down * (mm_split(mixing, pulled, 0, 0) + mm_exact_left(b, leaving)) + skip * d_mixed
    input_grad_ref[...] = d_x.astype(BF16)
    paired = jnp.where(lower, mm_split(pulled, pushed, 1, 1), 0.0)
    d_b = mm_exact_right(paired, c, 0, 0) + mm_split(pushed, leaving, 1, 1)
    d_c = mm_exact_right(paired, b) + mm_split(pulled, entering, 1, 1)
    pair_grad_ref[:, 0:STATE] = d_b.astype(BF16)
    pair_grad_ref[:, STATE : 2 * STATE] = d_c.astype(BF16)


VM = pl.BlockSpec(memory_space=pltpu.VMEM)
SM = pl.BlockSpec(memory_space=pltpu.SMEM)


def call(kernel, outs, args, specs=None, scratch=(), collective=None):
    extra = {} if collective is None else dict(collective_id=collective, has_side_effects=True)
    return pl.pallas_call(
        kernel,
        out_shape=[jax.ShapeDtypeStruct(shape, kind) for shape, kind in outs],
        in_specs=specs or [VM] * len(args),
        out_specs=[VM] * len(outs),
        scratch_shapes=list(scratch),
        compiler_params=pltpu.CompilerParams(vmem_limit_bytes=VMEM_LIMIT, **extra),
    )(*args)


def sems(*counts):
    return [pltpu.SemaphoreType.DMA((n,)) for n in counts for _ in range(2)]


def local(inputs, gates, pairs, steps, log_decay, skip, gain, out_weight, out_grad, order_ids):
    x, z, bc, dt, og = inputs[0], gates[0], pairs[0], steps[0], out_grad[0]
    decay, skip_row, gain_row = log_decay[None], skip[None], gain[None]
    grads, entering = call(
        forward_kernel,
        [((T, W), BF16), ((STATE, W), F32)],
        (order_ids, og, x, bc, dt, decay),
        [SM] + [VM] * 5,
        [pltpu.VMEM((SEQ, 16, 256), BF16)] * 2 + sems(SEQ) + StateExchange.SCRATCH,
        0,
    )
    gate_grad, normed, d_mixed, returns, sums = call(
        middle_kernel,
        [((T, W), BF16), ((T, W), BF16), ((T, W), F32), ((STATE, W), F32), ((2, W), F32)],
        (x, z, bc, dt, decay, skip_row, gain_row, out_weight, grads, entering),
    )
    tiny = pltpu.VMEM((8, W), F32)
    full, leaving, total = call(
        backward_kernel,
        [((W, W), BF16), ((STATE, W), F32), ((2, W), F32)],
        (normed, grads, returns, dt, decay, sums),
        None,
        [
            pltpu.VMEM((T, 512), BF16),
            pltpu.VMEM((T, W), BF16),
            pltpu.VMEM((512, W), F32),
            pltpu.VMEM((512, W), BF16),
            pltpu.VMEM((128, 512), F32),
            pltpu.VMEM((128, 512), F32),
            pltpu.VMEM((3, 128, 512), BF16),
            pltpu.VMEM((3, 128, 512), BF16),
            pltpu.VMEM((3, 32, 512), F32),
            pltpu.VMEM((3, 32, 512), F32),
            pltpu.VMEM((8, 16, 256), F32),
            pltpu.VMEM((7, 16, 256), F32),
            pltpu.VMEM((8, 16, 256), BF16),
            tiny, tiny, tiny, tiny, tiny,
            pltpu.VMEM((3, 8, W), F32),
            pltpu.VMEM((3, 8, W), F32),
            pltpu.VMEM((7, 8, W), F32),
        ]
        + sems(2, 4, 4, 4, 4, 8, 8, 4, 4, 4, 4, 8, 1, 4, 4, 8)
        + StateExchange.SCRATCH,
        1,
    )
    input_grad, pair_grad = call(
        final_kernel,
        [((T, W), BF16), ((T, 2 * STATE), BF16)],
        (x, bc, dt, decay, skip_row, d_mixed, entering, leaving),
    )
    skip_grad = jnp.sum(total[1].reshape(HEADS, W // HEADS), axis=1)
    return input_grad[None], gate_grad[None], pair_grad[None], full.astype(F32), total[0], skip_grad


def solution(mesh):
    token = P("dp", "seq", None)
    return jax.shard_map(
        local,
        mesh=mesh,
        in_specs=(token, token, token, P("dp", None, "seq"), P(), P(), P(), P(), token, P()),
        out_specs=(token, token, token, P(), P(), P()),
        check_vma=False,
    )
```

```python
import types

import jax
import jax.numpy as jnp
from jax import lax
from jax.experimental import pallas as pl
from jax.experimental.pallas import tpu as pltpu
from jax.sharding import PartitionSpec as P

F32 = jnp.float32
BF16 = jnp.bfloat16
MESH = pl.DeviceIdType.MESH
EPSILON = 1e-05
T = 256
W = 1024
HEADS = 16
STATE = 64
SEQ, NX, NY, NZ, GROUP = 64, 4, 4, 8, 16
VMEM_LIMIT = 56 * 1024 * 1024


def iota(shape, dim):
    return lax.broadcasted_iota(jnp.int32, shape, dim)


def mm(a, b, ca=1, cb=0):
    return lax.dot_general(a, b, (((ca,), (cb,)), ((), ())), preferred_element_type=F32)


def split(a):
    high = a.astype(BF16)
    return high, (a - high.astype(F32)).astype(BF16)


def mm_exact_left(a, b, ca=1, cb=0):
    high, low = split(b)
    return mm(a, high, ca, cb) + mm(a, low, ca, cb)


def mm_exact_right(a, b, ca=1, cb=0):
    high, low = split(a)
    return mm(high, b, ca, cb) + mm(low, b, ca, cb)


def mm_split(a, b, ca=1, cb=0):
    ah, al = split(a)
    bh, bl = split(b)
    return mm(ah, bh, ca, cb) + (mm(ah, bl, ca, cb) + mm(al, bh, ca, cb))


def terms(a):
    high = a.astype(BF16)
    rest = a - high.astype(F32)
    mid = rest.astype(BF16)
    return high, mid, (rest - mid.astype(F32)).astype(BF16)


def expand(small):
    spread = (iota((HEADS, W), 1) // (W // HEADS) == iota((HEADS, W), 0)).astype(F32).astype(BF16)
    high, mid, low = terms(small)
    return mm(high, spread) + (mm(mid, spread) + mm(low, spread))


def scales(steps, log_decay):
    token_steps = steps.T
    lower = (iota((T, T), 0) >= iota((T, T), 1)).astype(F32).astype(BF16)
    high, mid, low = terms(token_steps * (-jnp.exp(log_decay)))
    logs = mm(lower, high) + (mm(lower, mid) + mm(lower, low))
    mid = 0.5 * logs[T - 1 : T, :]
    down = expand(jnp.exp(mid - logs) * token_steps)
    half = expand(jnp.broadcast_to(jnp.exp(mid), (8, HEADS)))
    return jnp.exp(logs - mid), down, half


def place():
    s = lax.axis_index("seq")
    return s, lax.axis_index("dp"), s // GROUP, s % GROUP


def copy_to(src, dst, send, recv, seq, dp):
    return pltpu.make_async_remote_copy(
        src_ref=src, dst_ref=dst, send_sem=send, recv_sem=recv, device_id={"seq": seq, "dp": dp}, device_id_type=MESH
    )


def each(count, act, start=1):
    def body(i, carry):
        act(i)
        return carry

    lax.fori_loop(start, count, body, 0)


def far_first(count):
    return sorted(range(1, count), key=lambda i: -min(i, count - i))


def begin(copies):
    for one in copies:
        one.start()


def end(copies):
    for one in copies:
        one.wait()


def rows(i, size, base=0):
    return pl.ds(pl.multiple_of(base + i * size, size), size)


def dma(*count):
    return pltpu.SemaphoreType.DMA(count)


class StateExchange:
    def __init__(self, ref, wire, reverse):
        self.ref, self.reverse, self.wire = ref, reverse, wire
        self.s, self.x, self.y, m = place()
        self.m, self.z, self.core = m, m // 2, m % 2
        self.other = self.s + 1 - 2 * self.core
        self.early = self.core == (1 if reverse else 0)

    @staticmethod
    def scratch(wire, back):
        tiles = 5 if wire == F32 else 6
        return dict(
            stage=pltpu.VMEM((2, NZ, 4, 8, 128), F32),
            decay=pltpu.VMEM((8, 128), F32),
            peer=pltpu.VMEM((NZ, 4, 8, 128), F32),
            peer_decay=pltpu.VMEM((8, 128), F32),
            out=pltpu.VMEM((NZ, 8 * tiles, 128), wire),
            inc=pltpu.VMEM((NZ, 8 * tiles, 128), wire),
            fold=pltpu.VMEM((NZ, tiles, 8, 128), F32),
            tot=pltpu.VMEM((5, 8, 128), F32),
            tots=pltpu.VMEM((NY, 5, 8, 128), F32),
            ans=pltpu.VMEM((NZ, 32, 128), back),
            got=pltpu.VMEM((NZ, 32, 128), back),
            give=pltpu.VMEM((NZ, 4, 8, 128), F32),
            take=pltpu.VMEM((NZ, 4, 8, 128), F32),
            s0=dma(3),
            r0=dma(3),
            s1=dma(NZ),
            r1=dma(NZ),
            s2=dma(NY),
            r2=dma(NY),
            s3=dma(NZ),
            r3=dma(NZ),
        )

    def pair(self, k):
        r = self.ref
        src, dst = ((r.stage.at[1 - self.core], r.peer), (r.decay, r.peer_decay), (r.give, r.take))[k]
        return copy_to(src, dst, r.s0.at[k], r.r0.at[k], self.other, self.x)

    def along_z(self, src, dst, send, recv, i):
        to = (self.z + i) % NZ
        return copy_to(
            src.at[to], dst.at[self.z], send.at[i], recv.at[i], self.y * GROUP + to * 2 + self.core, self.x
        )

    def first(self, i):
        return self.along_z(self.ref.out, self.ref.inc, self.ref.s1, self.ref.r1, i)

    def second(self, i):
        r, to = self.ref, (self.y + i) % NY
        return copy_to(r.tot, r.tots.at[self.y], r.s2.at[i], r.r2.at[i], to * GROUP + self.m, self.x)

    def third(self, i):
        return self.along_z(self.ref.ans, self.ref.got, self.ref.s3, self.ref.r3, i)

    def start(self, state, decay):
        r = self.ref
        for b in range(8):
            lanes = slice(128 * b, 128 * b + 128)
            r.decay[b : b + 1] = decay[0:1, lanes]
            for k in range(4):
                for core in range(2):
                    at = 16 * k + 8 * core
                    r.stage[core, :, k, b, :] = state[at : at + 8, lanes]

    def share(self):
        begin([self.pair(1), self.pair(0)])

    def send(self):
        r = self.ref
        end([self.pair(1), self.pair(0)])
        own, peer = r.stage[pl.ds(self.core, 1)][0], r.peer[...]
        mine, theirs = r.decay[...], r.peer_decay[...]
        early = jnp.full((8, 128), self.early.astype(jnp.int32)) > 0
        own_factor, peer_factor = jnp.where(early, theirs, 1.0), jnp.where(early, 1.0, mine)
        r.fold[:, 0:4] = own_factor * own + peer_factor * peer
        both = mine * theirs
        if self.wire == F32:
            r.fold[:, 4] = jnp.broadcast_to(both, (NZ, 8, 128))
        else:
            high = both.astype(BF16).astype(F32)
            r.fold[:, 4] = jnp.broadcast_to(high, (NZ, 8, 128))
            r.fold[:, 5] = jnp.broadcast_to(both - high, (NZ, 8, 128))
        r.out[...] = r.fold[...].reshape(r.out.shape).astype(self.wire)
        begin([self.first(i) for i in far_first(NZ)])
        r.inc[pl.ds(self.z, 1)] = r.out[pl.ds(self.z, 1)]

    def fold(self):
        r = self.ref
        end([self.first(i) for i in far_first(NZ)])
        r.fold[...] = r.inc[...].astype(F32).reshape(r.fold.shape)
        total, decay = jnp.zeros((4, 8, 128), F32), jnp.ones((8, 128), F32)
        for j in range(NZ)[:: -1 if self.reverse else 1]:
            block = r.fold[j]
            r.fold[j, 0:4] = total
            r.fold[j, 4] = decay
            factor = block[4] if self.wire == F32 else block[4] + block[5]
            total, decay = factor[None] * total + block[0:4], factor * decay
        r.tot[0:4] = total
        r.tot[4] = decay
        begin([self.second(i) for i in far_first(NY)])
        r.tots[pl.ds(self.y, 1)] = r.tot[...][None]

    def answer(self):
        r = self.ref
        end([self.second(i) for i in far_first(NY)])
        before = jnp.zeros((4, 8, 128), F32)
        for j in range(NY)[:: -1 if self.reverse else 1]:
            reached = (self.y < j) if self.reverse else (self.y > j)
            flag = jnp.full((4, 8, 128), reached.astype(jnp.int32)) > 0
            before = jnp.where(flag, r.tots[j, 4][None] * before + r.tots[j, 0:4], before)
        answers = r.fold[:, 0:4] + r.fold[:, 4:5] * before[None]
        r.ans[...] = answers.reshape(r.ans.shape).astype(r.ans.dtype)
        begin([self.third(i) for i in far_first(NZ)])
        r.got[pl.ds(self.z, 1)] = r.ans[pl.ds(self.z, 1)]

    def halve(self):
        r = self.ref
        end([self.third(i) for i in far_first(NZ)])
        entering = r.got[...].astype(F32).reshape(NZ, 4, 8, 128)
        own, peer = r.stage[pl.ds(self.core, 1)][0], r.peer[...]
        early = jnp.full((NZ, 4, 8, 128), self.early.astype(jnp.int32)) > 0
        r.give[...] = jnp.where(early, r.decay[...] * entering + own, entering)
        begin([self.pair(2)])
        r.stage[pl.ds(self.core, 1)] = jnp.where(early, entering, r.peer_decay[...] * entering + peer)[None]

    def finish(self, state_ref, scale):
        r = self.ref
        end([self.pair(2)])
        r.stage[pl.ds(1 - self.core, 1)] = r.take[...][None]
        for b in range(8):
            lanes = slice(128 * b, 128 * b + 128)
            for k in range(4):
                for core in range(2):
                    at = 16 * k + 8 * core
                    state_ref[at : at + 8, lanes] = r.stage[core, :, k, b, :] * scale[:, lanes]


class Ring:
    def __init__(self, ref, me, device):
        self.ref, self.me, self.right, self.left = ref, me, device(1), device(3)

    @staticmethod
    def scratch():
        half, whole = pltpu.VMEM((64, 512), BF16), pltpu.VMEM((128, 512), BF16)
        return dict(
            in_left=half, in_right=half, to_right=half, to_left=half, from_left=whole, from_right=whole,
            s1=dma(6), r1=dma(6), s6=dma(6), r6=dma(6),
        )

    def one(self, k, src, dst, device, send, recv):
        return copy_to(src, dst, send.at[k], recv.at[k], *device)

    def start_sum(self, rough, lanes):
        r, me = self.ref, self.me
        far, right, left = 128 * ((me + 2) % 4), 128 * ((me + 1) % 4), 128 * ((me + 3) % 4)
        top, low = slice(0, 64), slice(64, 128)
        parts = (
            (rough.at[rows(0, 64, far), lanes], r.in_left, self.right),
            (rough.at[rows(1, 64, far), lanes], r.in_right, self.left),
            (rough.at[rows(1, 64, right), lanes], r.from_left.at[low], self.right),
            (rough.at[rows(0, 64, left), lanes], r.from_right.at[top], self.left),
            (r.to_right, r.from_left.at[top], self.right),
            (r.to_left, r.from_right.at[low], self.left),
        )
        self.sums = [self.one(k, *part, r.s1, r.r1) for k, part in enumerate(parts)]
        begin(self.sums[0:4])

    def pass_sum(self, mine, lanes):
        r, me = self.ref, self.me
        end(self.sums[0:1])
        r.to_right[...] = (mine[rows(0, 64, 128 * ((me + 1) % 4)), lanes] + r.in_left[...].astype(F32)).astype(BF16)
        begin(self.sums[4:5])
        end(self.sums[1:2])
        r.to_left[...] = (mine[rows(1, 64, 128 * ((me + 3) % 4)), lanes] + r.in_right[...].astype(F32)).astype(BF16)
        begin(self.sums[5:6])

    def end_sum(self, mine, lanes):
        r = self.ref
        end(self.sums[2:6])
        return mine[rows(self.me, 128), lanes] + (r.from_left[...].astype(F32) + r.from_right[...].astype(F32))

    def start_gather(self, full, base, lanes):
        r, me = self.ref, self.me

        def half(j, low):
            return full.at[rows(low, 64, base + 128 * ((me + j) % 4)), lanes]

        def send(k, j, low, device):
            return self.one(k, half(j, low), half(j, low), device, r.s6, r.r6)

        self.gathers = [
            send(0, 0, 0, self.right),
            send(1, 0, 1, self.left),
            send(2, 0, 1, self.right),
            send(3, 0, 0, self.left),
            send(4, 3, 0, self.right),
            send(5, 1, 1, self.left),
        ]
        begin(self.gathers[0:4])

    def pass_gather(self):
        end(self.gathers[0:1])
        begin(self.gathers[4:5])
        end(self.gathers[1:2])
        begin(self.gathers[5:6])


def buffers():
    full, half = pltpu.VMEM((T, W), F32), pltpu.VMEM((T, W), BF16)
    out = dict(
        x=half,
        z=half,
        og=half,
        bc=pltpu.VMEM((T, 2 * STATE), BF16),
        dt=pltpu.VMEM((HEADS, T), F32),
        w=pltpu.VMEM((W, W), BF16),
        load=dma(6),
        save=dma(20),
        swap_out=pltpu.VMEM((SEQ, 16, 256), BF16),
        swap_in=pltpu.VMEM((SEQ, 16, 256), BF16),
        swap_s=dma(SEQ),
        swap_r=dma(SEQ),
        grads=half,
        u=pltpu.VMEM((T, HEADS), F32),
        up=full,
        down=full,
        half=pltpu.VMEM((8, W), F32),
        skip=pltpu.VMEM((8, W), F32),
        pushed=full,
        mixing=pltpu.VMEM((T, T), F32),
        inner=full,
        active=full,
        slope=full,
        entering=pltpu.VMEM((STATE, W), F32),
        leaving=pltpu.VMEM((STATE, W), F32),
        inverse=pltpu.VMEM((T, 1), F32),
        unit=full,
        normed=half,
        d_normed=full,
        d_mixed=full,
        pulled=full,
        d_x=full,
        d_b=pltpu.VMEM((T, STATE), F32),
        gate_grad=half,
        input_grad=half,
        pair_grad=pltpu.VMEM((T, 2 * STATE), BF16),
        peer_normed=pltpu.VMEM((T, 512), BF16),
        peer_grads=half,
        pair_s=dma(2),
        pair_r=dma(2),
        mine=pltpu.VMEM((512, W), F32),
        rough=pltpu.VMEM((512, W), BF16),
        a1=pltpu.VMEM((128, 512), F32),
        b1=pltpu.VMEM((128, 512), F32),
        a1_out=pltpu.VMEM((128, 512), BF16),
        b1_out=pltpu.VMEM((128, 512), BF16),
        a2=pltpu.VMEM((3, 32, 512), BF16),
        b2=pltpu.VMEM((3, 32, 512), BF16),
        a2_s=dma(4), a2_r=dma(4), b2_s=dma(4), b2_r=dma(4),
        c1=pltpu.VMEM((8, 16, 256), F32),
        c3=pltpu.VMEM((7, 16, 256), F32),
        c3_s=dma(8), c3_r=dma(8), c4_s=dma(8), c4_r=dma(8),
        c4=pltpu.VMEM((8, 16, 256), BF16),
        a5_s=dma(4), a5_r=dma(4), b5_s=dma(4), b5_r=dma(4),
        full=pltpu.VMEM((W, W), BF16),
        last_s=dma(8), last_r=dma(8),
        sums=pltpu.VMEM((16, 128), F32),
    )
    rounds = [
        dict(
            mine=pltpu.VMEM((16, 128), F32), theirs=pltpu.VMEM((count - 1, 16, 128), F32), s=dma(count), r=dma(count)
        )
        for count in (2, NX, NY, NZ)
    ]
    return [out, StateExchange.scratch(*FORWARD), StateExchange.scratch(*BACKWARD), Ring.scratch(), Ring.scratch(), *rounds]


FORWARD, BACKWARD = (F32, F32), (F32, F32)
BUFFERS = buffers()


def kernel(
    orders, decay_ref, skip_ref, gain_ref, x_in, z_in, bc_in, dt_in, w_in, og_in,
    input_grad_out, gate_grad_out, pair_grad_out, full_out, total_out, *scratch,
):
    scratch = iter(scratch)
    ref, ref_f, ref_b, ring_a, ring_b, *rounds = [
        types.SimpleNamespace(**{key: next(scratch) for key in group}) for group in BUFFERS
    ]
    s, x, y, m = place()
    z, core = m // 2, m % 2
    other = s + 1 - 2 * core

    barrier = pltpu.get_barrier_semaphore()

    def hello(seq, dp):
        pl.semaphore_signal(barrier, inc=1, device_id=dict(seq=seq, dp=dp), device_id_type=MESH)

    operands = ((dt_in, ref.dt), (bc_in, ref.bc), (x_in, ref.x), (og_in, ref.og), (z_in, ref.z), (w_in, ref.w))
    loads = [pltpu.make_async_copy(src, dst, ref.load.at[k]) for k, (src, dst) in enumerate(operands)]
    begin(loads)
    each(SEQ, lambda i: hello((s + i) % SEQ, x))
    each(NX, lambda i: hello(s, (x + i) % NX))

    end(loads[0:1])
    ref.u[...], down, half = scales(ref.dt[...], decay_ref[...])
    ref.down[...], ref.half[...] = down, half
    end(loads[1:3])
    ref.pushed[...] = down * ref.x[...].astype(F32)
    forward = StateExchange(ref_f, FORWARD[0], False)
    b, c = ref.bc[:, 0:STATE], ref.bc[:, STATE : 2 * STATE]
    forward.start(half[0:1] * mm_exact_left(b, ref.pushed[...], 0, 0), half * half)
    pl.semaphore_wait(barrier, SEQ - 1 + NX - 1)
    forward.share()

    flip_rows = (orders[0] + orders[1]) % 2
    flip_columns = (orders[0] // 2 + orders[1] // 2 + s) % 2
    row = iota((4 * T, T), 0)
    device, quarter, line = row // 16, (row // 4) % 4, row % 4
    token = line * SEQ + jnp.where((line + flip_rows) % 2 == 0, device, SEQ - 1 - device)
    column = iota((4 * T, T), 1)
    end(loads[3:4])
    packed = jnp.zeros((4 * T, T), F32)
    for j in range(4):
        pick = jnp.where((token == column) & (quarter == j), 1.0, 0.0).astype(BF16)
        packed = packed + mm(pick, ref.og[:, 256 * j : 256 * j + 256])
    ref.swap_out[...] = packed.astype(BF16).reshape(SEQ, 16, 256)

    forward.send()

    def swap(i):
        to = (s + i) % SEQ
        return copy_to(ref.swap_out.at[to], ref.swap_in.at[s], ref.swap_s.at[i], ref.swap_r.at[i], to, x)

    each(SEQ, lambda i: swap(i).start())
    ref.swap_in[pl.ds(s, 1)] = ref.swap_out[pl.ds(s, 1)]

    lower = iota((T, T), 0) >= iota((T, T), 1)
    ref.mixing[...] = jnp.where(lower, mm(c, b, 1, 1), 0.0)
    ref.inner[...] = mm_split(ref.mixing[...], ref.pushed[...])
    ref.up[...] = expand(ref.u[...])
    ref.skip[...] = expand(jnp.broadcast_to(skip_ref[...], (8, HEADS)))
    forward.fold()
    end(loads[4:5])
    gate = ref.z[...].astype(F32)
    sigma = jax.nn.sigmoid(gate)
    ref.active[...] = gate * sigma
    ref.slope[...] = sigma * (1.0 + gate * (1.0 - sigma))
    forward.answer()
    forward.halve()

    each(SEQ, lambda i: swap(i).wait())
    arrived = ref.swap_in[...].reshape(4 * T, 256)
    at = iota((T, 4 * T), 0)
    source = jnp.where(flip_columns == 0, at, T - 1 - at)
    source = (source // 4) * 16 + source % 4
    column = iota((T, 4 * T), 1)
    for j in range(4):
        pick = jnp.where(source + 4 * j == column, 1.0, 0.0).astype(BF16)
        ref.grads[:, 256 * j : 256 * j + 256] = mm(pick, arrived).astype(BF16)
    share_grads = copy_to(ref.grads, ref.peer_grads, ref.pair_s.at[0], ref.pair_r.at[0], other, x)
    share_grads.start()

    forward.finish(ref.entering, ref.half[0:1])
    gain = gain_ref[...]
    mixed = ref.up[...] * (ref.inner[...] + mm_exact_left(c, ref.entering[...]))
    mixed = mixed + ref.skip[0:1] * ref.x[...].astype(F32)
    ref.inner[...] = mixed
    gated = mixed * ref.active[...]
    inverse = lax.rsqrt(jnp.mean(gated * gated, axis=1, keepdims=True) + EPSILON)
    ref.inverse[...] = inverse
    unit = gated * inverse
    ref.unit[...] = unit
    ref.normed[...] = (unit * gain).astype(BF16)

    share_normed = copy_to(
        ref.normed.at[:, rows(1 - core, 512)], ref.peer_normed, ref.pair_s.at[1], ref.pair_r.at[1], other, x
    )
    share_normed.start()
    ref.mine[...] = mm(ref.normed[:, rows(core, 512)], ref.grads[...], 0, 0)
    end([share_grads, share_normed])
    ref.mine[...] += mm(ref.peer_normed[...], ref.peer_grads[...], 0, 0)
    ref.rough[...] = ref.mine[...].astype(BF16)

    def along_x(i):
        return s, (x + i) % NX

    def along_y(i):
        return ((y + i) % NY) * GROUP + m, x

    def along_z(i):
        return y * GROUP + ((z + i) % NZ) * 2 + core, x

    def to_each(count, send, recv, peer, src, dst):
        return [copy_to(src(i), dst(i), send.at[i], recv.at[i], *peer(i)) for i in far_first(count)]

    left, right = slice(0, 512), slice(512, 1024)
    ring_a, ring_b = Ring(ring_a, x, along_x), Ring(ring_b, y, along_y)
    ring_a.start_sum(ref.rough, left)
    ring_b.start_sum(ref.rough, right)

    end(loads[5:6])
    d_normed = mm(ref.grads[...], ref.w[...], 1, 1)
    ref.d_normed[...] = d_normed
    unit = ref.unit[...]
    scaled = d_normed * gain
    d_gated = ref.inverse[...] * (scaled - unit * jnp.mean(scaled * unit, axis=1, keepdims=True))
    d_mixed = d_gated * ref.active[...]
    ref.d_mixed[...] = d_mixed
    ref.pulled[...] = ref.up[...] * d_mixed
    backward = StateExchange(ref_b, BACKWARD[0], True)
    half = ref.half[...]
    backward.start(half[0:1] * mm_exact_left(c, ref.pulled[...], 0, 0), half * half)
    backward.share()
    ring_a.pass_sum(ref.mine, left)
    ring_b.pass_sum(ref.mine, right)
    gain_sum = jnp.sum(ref.d_normed[...] * ref.unit[...], axis=0, keepdims=True)
    skip_sum = jnp.sum(ref.d_mixed[...] * ref.x[...].astype(F32), axis=0, keepdims=True)
    for k in range(8):
        lanes = slice(128 * k, 128 * k + 128)
        rounds[0].mine[k : k + 1] = gain_sum[:, lanes]
        rounds[0].mine[8 + k : 9 + k] = skip_sum[:, lanes]

    def sum_round(one, count, peer):
        return to_each(count, one.s, one.r, peer, lambda i: one.mine, lambda i: one.theirs.at[i - 1])

    def sum_end(one, copies):
        end(copies)
        total = one.mine[...]
        for i in range(len(copies)):
            total = total + one.theirs[i]
        return total

    sums = sum_round(rounds[0], 2, lambda i: (other, x))
    begin(sums)
    backward.send()
    saves = []

    def save(src, dst):
        saves.append(pltpu.make_async_copy(src, dst, ref.save.at[len(saves)]))
        saves[-1].start()

    d_gated = ref.inverse[...] * (
        ref.d_normed[...] * gain - ref.unit[...] * jnp.mean(ref.d_normed[...] * gain * ref.unit[...], axis=1, keepdims=True)
    )
    ref.gate_grad[...] = (d_gated * ref.inner[...] * ref.slope[...]).astype(BF16)
    save(ref.gate_grad, gate_grad_out)

    ref.a1[...] = ring_a.end_sum(ref.mine, left)
    ref.b1[...] = ring_b.end_sum(ref.mine, right)
    ref.a1_out[...] = ref.a1[...].astype(BF16)
    ref.b1_out[...] = ref.b1[...].astype(BF16)
    second = to_each(
        NY, ref.a2_s, ref.a2_r, along_y, lambda i: ref.a1_out.at[rows((y + i) % NY, 32)], lambda i: ref.a2.at[i - 1]
    ) + to_each(
        NX, ref.b2_s, ref.b2_r, along_x, lambda i: ref.b1_out.at[rows((x + i) % NX, 32)], lambda i: ref.b2.at[i - 1]
    )
    begin(second)
    backward.fold()
    rounds[1].mine[...] = sum_end(rounds[0], sums)
    sums = sum_round(rounds[1], NX, along_x)
    begin(sums)

    end(second)
    a2 = ref.a1[rows(y, 32), :] + (ref.a2[0].astype(F32) + ref.a2[1].astype(F32) + ref.a2[2].astype(F32))
    b2 = ref.b1[rows(x, 32), :] + (ref.b2[0].astype(F32) + ref.b2[1].astype(F32) + ref.b2[2].astype(F32))
    for k in range(4):
        part = (slice(16 * (k // 2), 16 * (k // 2) + 16), slice(256 * (k % 2), 256 * (k % 2) + 256))
        ref.c1[k] = a2[part]
        ref.c1[k + 4] = b2[part]
    third = to_each(
        NZ, ref.c3_s, ref.c3_r, along_z, lambda i: ref.c1.at[(z + i) % NZ], lambda i: ref.c3.at[i - 1]
    )
    begin(third)
    backward.answer()
    rounds[2].mine[...] = sum_end(rounds[1], sums)
    sums = sum_round(rounds[2], NY, along_y)
    begin(sums)
    pulled, pushed = ref.pulled[...], ref.pushed[...]
    paired = jnp.where(lower, mm_split(pulled, pushed, 1, 1), 0.0)
    ref.d_b[...] = mm_exact_right(paired, c, 0, 0)
    d_c = mm_exact_right(paired, b) + mm_split(pulled, ref.entering[...], 1, 1)
    ref.pair_grad[:, STATE : 2 * STATE] = d_c.astype(BF16)

    end(third)
    block = ref.c1[pl.ds(z, 1)][0]
    for i in range(NZ - 1):
        block = block + ref.c3[i]
    ref.c4[pl.ds(z, 1)] = block.astype(BF16)[None]
    mine = ref.c4.at[z]
    fourth = to_each(NZ, ref.c4_s, ref.c4_r, along_z, lambda i: mine, lambda i: mine)
    begin(fourth)
    backward.halve()
    rounds[3].mine[...] = sum_end(rounds[2], sums)
    sums = sum_round(rounds[3], NZ, along_z)
    begin(sums)
    ref.d_x[...] = mm_split(ref.mixing[...], ref.pulled[...], 0, 0)

    end(fourth)
    full, base = ref.full, core * 512
    for k in range(4):
        lanes = slice(256 * (k % 2), 256 * (k % 2) + 256)
        full[rows(k // 2, 16, base + 128 * x + 32 * y), lanes] = ref.c4[k]
        lanes = slice(512 + 256 * (k % 2), 512 + 256 * (k % 2) + 256)
        full[rows(k // 2, 16, base + 128 * y + 32 * x), lanes] = ref.c4[k + 4]
    at_a = full.at[rows(y, 32, base + 128 * x), left]
    at_b = full.at[rows(x, 32, base + 128 * y), right]
    fifth = to_each(NY, ref.a5_s, ref.a5_r, along_y, lambda i: at_a, lambda i: at_a) + to_each(
        NX, ref.b5_s, ref.b5_r, along_x, lambda i: at_b, lambda i: at_b
    )
    begin(fifth)
    backward.finish(ref.leaving, ref.half[0:1])
    end(fifth)
    ring_a.start_gather(full, base, left)
    ring_b.start_gather(full, base, right)

    last, others = [], []

    def hand_over(index, lanes):
        k, at = len(last), full.at[rows(index % 4, 128, base), lanes]
        last.append(copy_to(at, at, ref.last_s.at[k], ref.last_r.at[k], other, x))
        last[-1].start()
        save(at, full_out.at[rows(index % 4, 128, base), lanes])
        others.append((rows(index % 4, 128, 512 - base), lanes))

    hand_over(x, left)
    hand_over(y, right)
    leaving = ref.leaving[...]
    ref.pair_grad[:, 0:STATE] = (ref.d_b[...] + mm_split(ref.pushed[...], leaving, 1, 1)).astype(BF16)
    save(ref.pair_grad, pair_grad_out)
    ring_a.pass_gather()
    ring_b.pass_gather()
    ref.input_grad[...] = (
        ref.down[...] * (ref.d_x[...] + mm_exact_left(b, leaving)) + ref.skip[0:1] * ref.d_mixed[...]
    ).astype(BF16)
    save(ref.input_grad, input_grad_out)
    end([ring_a.gathers[2]])
    hand_over(x + 3, left)
    end([ring_b.gathers[2]])
    hand_over(y + 3, right)
    end([ring_a.gathers[3]])
    hand_over(x + 1, left)
    end([ring_b.gathers[3]])
    hand_over(y + 1, right)
    ref.sums[...] = sum_end(rounds[3], sums)
    save(ref.sums, total_out)
    end(ring_a.gathers[4:6])
    hand_over(x + 2, left)
    end(ring_b.gathers[4:6])
    hand_over(y + 2, right)
    for one, at in zip(last, others):
        one.wait()
        save(full.at[at], full_out.at[at])
    end(saves)


PARTS = 8


def widen(
    total, full_in, input_grad_in, gate_grad_in, pair_grad_in,
    full_out, gain, skip, input_grad_out, gate_grad_out, pair_grad_out,
    narrow, wide, token_a, token_b, pair, loads, saves, moves, moved_on,
):
    moved = ((input_grad_in, token_a, input_grad_out), (gate_grad_in, token_b, gate_grad_out), (pair_grad_in, pair, pair_grad_out))
    fetch = [pltpu.make_async_copy(src, via, moves.at[k]) for k, (src, via, _) in enumerate(moved)]
    store = [pltpu.make_async_copy(via, dst, moved_on.at[k]) for k, (_, via, dst) in enumerate(moved)]
    size = W // PARTS
    at = [pl.ds(size * k, size) for k in range(PARTS)]
    loaded = [pltpu.make_async_copy(full_in.at[at[k]], narrow.at[at[k]], loads.at[k]) for k in range(PARTS)]
    saved = [pltpu.make_async_copy(wide.at[at[k]], full_out.at[at[k]], saves.at[k]) for k in range(PARTS)]
    begin(loaded)
    begin(fetch)
    for k in range(8):
        gain[0:1, 128 * k : 128 * k + 128] = total[k : k + 1]
    lane, head = iota((8, 128), 1), iota((8, HEADS), 1)
    first = jnp.sum(jnp.where(lane < 64, total[8:16], 0.0), axis=1, keepdims=True)
    second = jnp.sum(jnp.where(lane < 64, 0.0, total[8:16]), axis=1, keepdims=True)
    both = jnp.where(head % 2 == 0, first, second)
    skip[...] = jnp.sum(jnp.where(head // 2 == iota((8, HEADS), 0), both, 0.0), axis=0, keepdims=True)
    for k in range(PARTS):
        loaded[k].wait()
        wide[at[k], :] = narrow[at[k], :].astype(F32)
        saved[k].start()
    for one, two in zip(fetch, store):
        one.wait()
        two.start()
    end(saved)
    end(store)


ANY = pl.BlockSpec(memory_space=pl.ANY)
VM = pl.BlockSpec(memory_space=pltpu.VMEM)
SM = pl.BlockSpec(memory_space=pltpu.SMEM)


def local(inputs, gates, pairs, steps, log_decay, skip, gain, out_weight, out_grad, order_ids):
    token, pair = jax.ShapeDtypeStruct((T, W), BF16), jax.ShapeDtypeStruct((T, 2 * STATE), BF16)
    input_grad, gate_grad, pair_grad, full, total = pl.pallas_call(
        kernel,
        out_shape=[token, token, pair, jax.ShapeDtypeStruct((W, W), BF16), jax.ShapeDtypeStruct((16, 128), F32)],
        in_specs=[SM, VM, VM, VM] + [ANY] * 6,
        out_specs=[ANY] * 5,
        scratch_shapes=[one for group in BUFFERS for one in group.values()],
        compiler_params=pltpu.CompilerParams(vmem_limit_bytes=VMEM_LIMIT, collective_id=0, has_side_effects=True),
    )(
        order_ids, log_decay[None], skip[None], gain[None], inputs[0], gates[0], pairs[0], steps[0], out_weight, out_grad[0]
    )

    weight_grad, gain_grad, skip_grad, input_grad, gate_grad, pair_grad = pl.pallas_call(
        widen,
        out_shape=[
            jax.ShapeDtypeStruct((W, W), F32),
            jax.ShapeDtypeStruct((1, W), F32),
            jax.ShapeDtypeStruct((1, HEADS), F32),
            token,
            token,
            pair,
        ],
        in_specs=[VM] + [ANY] * 4,
        out_specs=[ANY, VM, VM, ANY, ANY, ANY],
        scratch_shapes=[
            pltpu.VMEM((W, W), BF16), pltpu.VMEM((W, W), F32), pltpu.VMEM((T, W), BF16), pltpu.VMEM((T, W), BF16),
            pltpu.VMEM((T, 2 * STATE), BF16), dma(PARTS), dma(PARTS), dma(3), dma(3),
        ],
        compiler_params=pltpu.CompilerParams(vmem_limit_bytes=VMEM_LIMIT),
    )(total, full, input_grad, gate_grad, pair_grad)
    return input_grad[None], gate_grad[None], pair_grad[None], weight_grad, gain_grad[0], skip_grad[0]


def solution(mesh):
    token = P("dp", "seq", None)
    return jax.shard_map(
        local,
        mesh=mesh,
        in_specs=(token, token, token, P("dp", None, "seq"), P(), P(), P(), P(), token, P()),
        out_specs=(token, token, token, P(), P(), P()),
        check_vma=False,
    )
```

```python
import types

import jax
import jax.numpy as jnp
from jax import lax
from jax.experimental import pallas as pl
from jax.experimental.pallas import tpu as pltpu
from jax.sharding import PartitionSpec as P

F32 = jnp.float32
BF16 = jnp.bfloat16
MESH = pl.DeviceIdType.MESH
EPSILON = 1e-05
T = 256
W = 1024
HEADS = 16
STATE = 64
SEQ, NX, NY, NZ, GROUP = 64, 4, 4, 8, 16
VMEM_LIMIT = 56 * 1024 * 1024


def iota(shape, dim):
    return lax.broadcasted_iota(jnp.int32, shape, dim)


def mm(a, b, ca=1, cb=0):
    return lax.dot_general(a, b, (((ca,), (cb,)), ((), ())), preferred_element_type=F32)


def split(a):
    high = a.astype(BF16)
    return high, (a - high.astype(F32)).astype(BF16)


def mm_exact_left(a, b, ca=1, cb=0):
    high, low = split(b)
    return mm(a, high, ca, cb) + mm(a, low, ca, cb)


def mm_exact_right(a, b, ca=1, cb=0):
    high, low = split(a)
    return mm(high, b, ca, cb) + mm(low, b, ca, cb)


def mm_split(a, b, ca=1, cb=0):
    ah, al = split(a)
    bh, bl = split(b)
    return mm(ah, bh, ca, cb) + (mm(ah, bl, ca, cb) + mm(al, bh, ca, cb))


def terms(a):
    high = a.astype(BF16)
    rest = a - high.astype(F32)
    mid = rest.astype(BF16)
    return high, mid, (rest - mid.astype(F32)).astype(BF16)


def expand(small):
    spread = (iota((HEADS, W), 1) // (W // HEADS) == iota((HEADS, W), 0)).astype(F32).astype(BF16)
    high, mid, low = terms(small)
    return mm(high, spread) + (mm(mid, spread) + mm(low, spread))


def scales(steps, log_decay):
    token_steps = steps.T
    lower = (iota((T, T), 0) >= iota((T, T), 1)).astype(F32).astype(BF16)
    high, mid, low = terms(token_steps * (-jnp.exp(log_decay)))
    logs = mm(lower, high) + (mm(lower, mid) + mm(lower, low))
    mid = 0.5 * logs[T - 1 : T, :]
    down = expand(jnp.exp(mid - logs) * token_steps)
    half = expand(jnp.broadcast_to(jnp.exp(mid), (8, HEADS)))
    return jnp.exp(logs - mid), down, half


def place():
    s = lax.axis_index("seq")
    return s, lax.axis_index("dp"), s // GROUP, s % GROUP


def copy_to(src, dst, send, recv, seq, dp):
    return pltpu.make_async_remote_copy(
        src_ref=src, dst_ref=dst, send_sem=send, recv_sem=recv, device_id={"seq": seq, "dp": dp}, device_id_type=MESH
    )


def each(count, act, start=1):
    def body(i, carry):
        act(i)
        return carry

    lax.fori_loop(start, count, body, 0)


def far_first(count):
    return sorted(range(1, count), key=lambda i: -min(i, count - i))


def begin(copies):
    for one in copies:
        one.start()


def end(copies):
    for one in copies:
        one.wait()


def rows(i, size, base=0):
    return pl.ds(pl.multiple_of(base + i * size, size), size)


def dma(*count):
    return pltpu.SemaphoreType.DMA(count)


class StateExchange:
    def __init__(self, ref, wire, reverse):
        self.ref, self.reverse, self.wire = ref, reverse, wire
        self.s, self.x, self.y, m = place()
        self.m, self.z, self.core = m, m // 2, m % 2
        self.other = self.s + 1 - 2 * self.core
        self.early = self.core == (1 if reverse else 0)

    @staticmethod
    def scratch(wire, back):
        tiles = 5 if wire == F32 else 6
        return dict(
            stage=pltpu.VMEM((2, NZ, 4, 8, 128), F32),
            decay=pltpu.VMEM((8, 128), F32),
            peer=pltpu.VMEM((NZ, 4, 8, 128), F32),
            peer_decay=pltpu.VMEM((8, 128), F32),
            out=pltpu.VMEM((NZ, 8 * tiles, 128), wire),
            inc=pltpu.VMEM((NZ, 8 * tiles, 128), wire),
            fold=pltpu.VMEM((NZ, tiles, 8, 128), F32),
            tot=pltpu.VMEM((5, 8, 128), F32),
            tots=pltpu.VMEM((NY, 5, 8, 128), F32),
            ans=pltpu.VMEM((NZ, 32, 128), back),
            got=pltpu.VMEM((NZ, 32, 128), back),
            give=pltpu.VMEM((NZ, 4, 8, 128), F32),
            take=pltpu.VMEM((NZ, 4, 8, 128), F32),
            s0=dma(3),
            r0=dma(3),
            s1=dma(NZ),
            r1=dma(NZ),
            s2=dma(NY),
            r2=dma(NY),
            s3=dma(NZ),
            r3=dma(NZ),
        )

    def pair(self, k):
        r = self.ref
        src, dst = ((r.stage.at[1 - self.core], r.peer), (r.decay, r.peer_decay), (r.give, r.take))[k]
        return copy_to(src, dst, r.s0.at[k], r.r0.at[k], self.other, self.x)

    def along_z(self, src, dst, send, recv, i):
        to = (self.z + i) % NZ
        return copy_to(
            src.at[to], dst.at[self.z], send.at[i], recv.at[i], self.y * GROUP + to * 2 + self.core, self.x
        )

    def first(self, i):
        return self.along_z(self.ref.out, self.ref.inc, self.ref.s1, self.ref.r1, i)

    def second(self, i):
        r, to = self.ref, (self.y + i) % NY
        return copy_to(r.tot, r.tots.at[self.y], r.s2.at[i], r.r2.at[i], to * GROUP + self.m, self.x)

    def third(self, i):
        return self.along_z(self.ref.ans, self.ref.got, self.ref.s3, self.ref.r3, i)

    def start(self, state, decay):
        r = self.ref
        for b in range(8):
            lanes = slice(128 * b, 128 * b + 128)
            r.decay[b : b + 1] = decay[0:1, lanes]
            for k in range(4):
                for core in range(2):
                    at = 16 * k + 8 * core
                    r.stage[core, :, k, b, :] = state[at : at + 8, lanes]

    def share(self):
        begin([self.pair(1), self.pair(0)])

    def send(self):
        r = self.ref
        end([self.pair(1), self.pair(0)])
        own, peer = r.stage[pl.ds(self.core, 1)][0], r.peer[...]
        mine, theirs = r.decay[...], r.peer_decay[...]
        early = jnp.full((8, 128), self.early.astype(jnp.int32)) > 0
        own_factor, peer_factor = jnp.where(early, theirs, 1.0), jnp.where(early, 1.0, mine)
        r.fold[:, 0:4] = own_factor * own + peer_factor * peer
        both = mine * theirs
        if self.wire == F32:
            r.fold[:, 4] = jnp.broadcast_to(both, (NZ, 8, 128))
        else:
            high = both.astype(BF16).astype(F32)
            r.fold[:, 4] = jnp.broadcast_to(high, (NZ, 8, 128))
            r.fold[:, 5] = jnp.broadcast_to(both - high, (NZ, 8, 128))
        r.out[...] = r.fold[...].reshape(r.out.shape).astype(self.wire)
        begin([self.first(i) for i in far_first(NZ)])
        r.inc[pl.ds(self.z, 1)] = r.out[pl.ds(self.z, 1)]

    def fold(self):
        r = self.ref
        end([self.first(i) for i in far_first(NZ)])
        r.fold[...] = r.inc[...].astype(F32).reshape(r.fold.shape)
        total, decay = jnp.zeros((4, 8, 128), F32), jnp.ones((8, 128), F32)
        for j in range(NZ)[:: -1 if self.reverse else 1]:
            block = r.fold[j]
            r.fold[j, 0:4] = total
            r.fold[j, 4] = decay
            factor = block[4] if self.wire == F32 else block[4] + block[5]
            total, decay = factor[None] * total + block[0:4], factor * decay
        r.tot[0:4] = total
        r.tot[4] = decay
        begin([self.second(i) for i in far_first(NY)])
        r.tots[pl.ds(self.y, 1)] = r.tot[...][None]

    def answer(self):
        r = self.ref
        end([self.second(i) for i in far_first(NY)])
        before = jnp.zeros((4, 8, 128), F32)
        for j in range(NY)[:: -1 if self.reverse else 1]:
            reached = (self.y < j) if self.reverse else (self.y > j)
            flag = jnp.full((4, 8, 128), reached.astype(jnp.int32)) > 0
            before = jnp.where(flag, r.tots[j, 4][None] * before + r.tots[j, 0:4], before)
        answers = r.fold[:, 0:4] + r.fold[:, 4:5] * before[None]
        r.ans[...] = answers.reshape(r.ans.shape).astype(r.ans.dtype)
        begin([self.third(i) for i in far_first(NZ)])
        r.got[pl.ds(self.z, 1)] = r.ans[pl.ds(self.z, 1)]

    def halve(self):
        r = self.ref
        end([self.third(i) for i in far_first(NZ)])
        entering = r.got[...].astype(F32).reshape(NZ, 4, 8, 128)
        own, peer = r.stage[pl.ds(self.core, 1)][0], r.peer[...]
        early = jnp.full((NZ, 4, 8, 128), self.early.astype(jnp.int32)) > 0
        r.give[...] = jnp.where(early, r.decay[...] * entering + own, entering)
        begin([self.pair(2)])
        r.stage[pl.ds(self.core, 1)] = jnp.where(early, entering, r.peer_decay[...] * entering + peer)[None]

    def finish(self, state_ref, scale):
        r = self.ref
        end([self.pair(2)])
        r.stage[pl.ds(1 - self.core, 1)] = r.take[...][None]
        for b in range(8):
            lanes = slice(128 * b, 128 * b + 128)
            for k in range(4):
                for core in range(2):
                    at = 16 * k + 8 * core
                    state_ref[at : at + 8, lanes] = r.stage[core, :, k, b, :] * scale[:, lanes]


class Ring:
    def __init__(self, ref, me, device):
        self.ref, self.me, self.right, self.left = ref, me, device(1), device(3)

    @staticmethod
    def scratch():
        half, whole = pltpu.VMEM((64, 512), BF16), pltpu.VMEM((128, 512), BF16)
        return dict(
            in_left=half, in_right=half, to_right=half, to_left=half, from_left=whole, from_right=whole,
            s1=dma(6), r1=dma(6), s6=dma(6), r6=dma(6),
        )

    def one(self, k, src, dst, device, send, recv):
        return copy_to(src, dst, send.at[k], recv.at[k], *device)

    def start_sum(self, rough, lanes):
        r, me = self.ref, self.me
        far, right, left = 128 * ((me + 2) % 4), 128 * ((me + 1) % 4), 128 * ((me + 3) % 4)
        top, low = slice(0, 64), slice(64, 128)
        parts = (
            (rough.at[rows(0, 64, far), lanes], r.in_left, self.right),
            (rough.at[rows(1, 64, far), lanes], r.in_right, self.left),
            (rough.at[rows(1, 64, right), lanes], r.from_left.at[low], self.right),
            (rough.at[rows(0, 64, left), lanes], r.from_right.at[top], self.left),
            (r.to_right, r.from_left.at[top], self.right),
            (r.to_left, r.from_right.at[low], self.left),
        )
        self.sums = [self.one(k, *part, r.s1, r.r1) for k, part in enumerate(parts)]
        begin(self.sums[0:4])

    def pass_sum(self, mine, lanes):
        r, me = self.ref, self.me
        end(self.sums[0:1])
        r.to_right[...] = (mine[rows(0, 64, 128 * ((me + 1) % 4)), lanes] + r.in_left[...].astype(F32)).astype(BF16)
        begin(self.sums[4:5])
        end(self.sums[1:2])
        r.to_left[...] = (mine[rows(1, 64, 128 * ((me + 3) % 4)), lanes] + r.in_right[...].astype(F32)).astype(BF16)
        begin(self.sums[5:6])

    def end_sum(self, mine, lanes):
        r = self.ref
        end(self.sums[2:6])
        return mine[rows(self.me, 128), lanes] + (r.from_left[...].astype(F32) + r.from_right[...].astype(F32))

    def start_gather(self, full, base, lanes):
        r, me = self.ref, self.me

        def half(j, low):
            return full.at[rows(low, 64, base + 128 * ((me + j) % 4)), lanes]

        def send(k, j, low, device):
            return self.one(k, half(j, low), half(j, low), device, r.s6, r.r6)

        self.gathers = [
            send(0, 0, 0, self.right),
            send(1, 0, 1, self.left),
            send(2, 0, 1, self.right),
            send(3, 0, 0, self.left),
            send(4, 3, 0, self.right),
            send(5, 1, 1, self.left),
        ]
        begin(self.gathers[0:4])

    def pass_gather(self):
        end(self.gathers[0:1])
        begin(self.gathers[4:5])
        end(self.gathers[1:2])
        begin(self.gathers[5:6])


def buffers():
    full, half = pltpu.VMEM((T, W), F32), pltpu.VMEM((T, W), BF16)
    out = dict(
        x=half,
        z=half,
        og=half,
        bc=pltpu.VMEM((T, 2 * STATE), BF16),
        dt=pltpu.VMEM((HEADS, T), F32),
        w=pltpu.VMEM((W, W), BF16),
        entered=pltpu.SemaphoreType.REGULAR,
        load=dma(6),
        swap_out=pltpu.VMEM((SEQ, 16, 256), BF16),
        swap_in=pltpu.VMEM((SEQ, 16, 256), BF16),
        swap_s=dma(SEQ),
        swap_r=dma(SEQ),
        grads=half,
        u=pltpu.VMEM((T, HEADS), F32),
        up=full,
        down=full,
        half=pltpu.VMEM((8, W), F32),
        skip=pltpu.VMEM((8, W), F32),
        pushed=full,
        mixing=pltpu.VMEM((T, T), F32),
        inner=full,
        active=full,
        slope=full,
        entering=pltpu.VMEM((STATE, W), F32),
        leaving=pltpu.VMEM((STATE, W), F32),
        inverse=pltpu.VMEM((T, 1), F32),
        unit=full,
        normed=half,
        d_normed=full,
        d_mixed=full,
        pulled=full,
        d_x=full,
        d_b=pltpu.VMEM((T, STATE), F32),
        peer_normed=pltpu.VMEM((T, 512), BF16),
        peer_grads=half,
        pair_s=dma(2),
        pair_r=dma(2),
        mine=pltpu.VMEM((512, W), F32),
        rough=pltpu.VMEM((512, W), BF16),
        a1=pltpu.VMEM((128, 512), F32),
        b1=pltpu.VMEM((128, 512), F32),
        a1_out=pltpu.VMEM((128, 512), BF16),
        b1_out=pltpu.VMEM((128, 512), BF16),
        a2=pltpu.VMEM((3, 32, 512), BF16),
        b2=pltpu.VMEM((3, 32, 512), BF16),
        a2_s=dma(4), a2_r=dma(4), b2_s=dma(4), b2_r=dma(4),
        c1=pltpu.VMEM((8, 16, 256), F32),
        c3=pltpu.VMEM((7, 16, 256), F32),
        c3_s=dma(8), c3_r=dma(8), c4_s=dma(8), c4_r=dma(8),
        c4=pltpu.VMEM((8, 16, 256), BF16),
        a5_s=dma(4), a5_r=dma(4), b5_s=dma(4), b5_r=dma(4),
        last_s=dma(8), last_r=dma(8),
    )
    rounds = [
        dict(
            mine=pltpu.VMEM((16, 128), F32), theirs=pltpu.VMEM((count - 1, 16, 128), F32), s=dma(count), r=dma(count)
        )
        for count in (2, NX, NY, NZ)
    ]
    return [out, StateExchange.scratch(*FORWARD), StateExchange.scratch(*BACKWARD), Ring.scratch(), Ring.scratch(), *rounds]


FORWARD, BACKWARD = (F32, F32), (F32, F32)
BUFFERS = buffers()


def kernel(
    orders, decay_ref, skip_ref, gain_ref, x_in, z_in, bc_in, dt_in, w_in, og_in,
    input_grad, gate_grad, pair_grad, full, total, *scratch,
):
    scratch = iter(scratch)
    ref, ref_f, ref_b, ring_a, ring_b, *rounds = [
        types.SimpleNamespace(**{key: next(scratch) for key in group}) for group in BUFFERS
    ]
    s, x, y, m = place()
    z, core = m // 2, m % 2
    other = s + 1 - 2 * core

    barrier = pltpu.get_barrier_semaphore()

    def hello(seq, dp):
        pl.semaphore_signal(barrier, inc=1, device_id=dict(seq=seq, dp=dp), device_id_type=MESH)

    operands = ((dt_in, ref.dt), (bc_in, ref.bc), (x_in, ref.x), (og_in, ref.og), (z_in, ref.z), (w_in, ref.w))
    loads = [pltpu.make_async_copy(src, dst, ref.load.at[k]) for k, (src, dst) in enumerate(operands)]
    begin(loads)
    for i in far_first(GROUP):
        hello(y * GROUP + (m + i) % GROUP, x)
    for i in far_first(NY):
        hello(((y + i) % NY) * GROUP + m, x)
    for i in far_first(NX):
        hello(s, (x + i) % NX)

    end(loads[0:1])
    ref.u[...], down, half = scales(ref.dt[...], decay_ref[...])
    ref.down[...], ref.half[...] = down, half
    end(loads[1:3])
    ref.pushed[...] = down * ref.x[...].astype(F32)
    forward = StateExchange(ref_f, FORWARD[0], False)
    b, c = ref.bc[:, 0:STATE], ref.bc[:, STATE : 2 * STATE]
    forward.start(half[0:1] * mm_exact_left(b, ref.pushed[...], 0, 0), half * half)
    pl.semaphore_wait(barrier, GROUP - 1 + NY - 1 + NX - 1)
    for i in far_first(NY):
        pl.semaphore_signal(
            ref.entered, inc=1, device_id=dict(seq=((y + i) % NY) * GROUP + m, dp=x), device_id_type=MESH
        )
    forward.share()

    flip_rows = (orders[0] + orders[1]) % 2
    flip_columns = (orders[0] // 2 + orders[1] // 2 + s) % 2
    row = iota((4 * T, T), 0)
    device, quarter, line = row // 16, (row // 4) % 4, row % 4
    token = line * SEQ + jnp.where((line + flip_rows) % 2 == 0, device, SEQ - 1 - device)
    column = iota((4 * T, T), 1)
    end(loads[3:4])
    packed = jnp.zeros((4 * T, T), F32)
    for j in range(4):
        pick = jnp.where((token == column) & (quarter == j), 1.0, 0.0).astype(BF16)
        packed = packed + mm(pick, ref.og[:, 256 * j : 256 * j + 256])
    ref.swap_out[...] = packed.astype(BF16).reshape(SEQ, 16, 256)

    forward.send()

    pl.semaphore_wait(ref.entered, NY - 1)

    def swap(i):
        to = (s + i) % SEQ
        return copy_to(ref.swap_out.at[to], ref.swap_in.at[s], ref.swap_s.at[i], ref.swap_r.at[i], to, x)

    each(SEQ, lambda i: swap(i).start())
    ref.swap_in[pl.ds(s, 1)] = ref.swap_out[pl.ds(s, 1)]

    lower = iota((T, T), 0) >= iota((T, T), 1)
    ref.mixing[...] = jnp.where(lower, mm(c, b, 1, 1), 0.0)
    ref.inner[...] = mm_split(ref.mixing[...], ref.pushed[...])
    ref.up[...] = expand(ref.u[...])
    ref.skip[...] = expand(jnp.broadcast_to(skip_ref[...], (8, HEADS)))
    forward.fold()
    end(loads[4:5])
    gate = ref.z[...].astype(F32)
    sigma = jax.nn.sigmoid(gate)
    ref.active[...] = gate * sigma
    ref.slope[...] = sigma * (1.0 + gate * (1.0 - sigma))
    forward.answer()
    forward.halve()

    each(SEQ, lambda i: swap(i).wait())
    arrived = ref.swap_in[...].reshape(4 * T, 256)
    at = iota((T, 4 * T), 0)
    source = jnp.where(flip_columns == 0, at, T - 1 - at)
    source = (source // 4) * 16 + source % 4
    column = iota((T, 4 * T), 1)
    for j in range(4):
        pick = jnp.where(source + 4 * j == column, 1.0, 0.0).astype(BF16)
        ref.grads[:, 256 * j : 256 * j + 256] = mm(pick, arrived).astype(BF16)
    share_grads = copy_to(ref.grads, ref.peer_grads, ref.pair_s.at[0], ref.pair_r.at[0], other, x)
    share_grads.start()

    forward.finish(ref.entering, ref.half[0:1])
    gain = gain_ref[...]
    mixed = ref.up[...] * (ref.inner[...] + mm_exact_left(c, ref.entering[...]))
    mixed = mixed + ref.skip[0:1] * ref.x[...].astype(F32)
    ref.inner[...] = mixed
    gated = mixed * ref.active[...]
    inverse = lax.rsqrt(jnp.mean(gated * gated, axis=1, keepdims=True) + EPSILON)
    ref.inverse[...] = inverse
    unit = gated * inverse
    ref.unit[...] = unit
    ref.normed[...] = (unit * gain).astype(BF16)

    share_normed = copy_to(
        ref.normed.at[:, rows(1 - core, 512)], ref.peer_normed, ref.pair_s.at[1], ref.pair_r.at[1], other, x
    )
    share_normed.start()
    ref.mine[...] = mm(ref.normed[:, rows(core, 512)], ref.grads[...], 0, 0)
    end([share_grads, share_normed])
    ref.mine[...] += mm(ref.peer_normed[...], ref.peer_grads[...], 0, 0)
    ref.rough[...] = ref.mine[...].astype(BF16)

    def along_x(i):
        return s, (x + i) % NX

    def along_y(i):
        return ((y + i) % NY) * GROUP + m, x

    def along_z(i):
        return y * GROUP + ((z + i) % NZ) * 2 + core, x

    def to_each(count, send, recv, peer, src, dst):
        return [copy_to(src(i), dst(i), send.at[i], recv.at[i], *peer(i)) for i in far_first(count)]

    left, right = slice(0, 512), slice(512, 1024)
    ring_a, ring_b = Ring(ring_a, x, along_x), Ring(ring_b, y, along_y)
    ring_a.start_sum(ref.rough, left)
    ring_b.start_sum(ref.rough, right)

    end(loads[5:6])
    d_normed = mm(ref.grads[...], ref.w[...], 1, 1)
    ref.d_normed[...] = d_normed
    unit = ref.unit[...]
    scaled = d_normed * gain
    d_gated = ref.inverse[...] * (scaled - unit * jnp.mean(scaled * unit, axis=1, keepdims=True))
    d_mixed = d_gated * ref.active[...]
    ref.d_mixed[...] = d_mixed
    ref.pulled[...] = ref.up[...] * d_mixed
    backward = StateExchange(ref_b, BACKWARD[0], True)
    half = ref.half[...]
    backward.start(half[0:1] * mm_exact_left(c, ref.pulled[...], 0, 0), half * half)
    backward.share()
    ring_a.pass_sum(ref.mine, left)
    ring_b.pass_sum(ref.mine, right)
    gain_sum = jnp.sum(ref.d_normed[...] * ref.unit[...], axis=0, keepdims=True)
    skip_sum = jnp.sum(ref.d_mixed[...] * ref.x[...].astype(F32), axis=0, keepdims=True)
    for k in range(8):
        lanes = slice(128 * k, 128 * k + 128)
        rounds[0].mine[k : k + 1] = gain_sum[:, lanes]
        rounds[0].mine[8 + k : 9 + k] = skip_sum[:, lanes]

    def sum_round(one, count, peer):
        return to_each(count, one.s, one.r, peer, lambda i: one.mine, lambda i: one.theirs.at[i - 1])

    def sum_end(one, copies):
        end(copies)
        total = one.mine[...]
        for i in range(len(copies)):
            total = total + one.theirs[i]
        return total

    sums = sum_round(rounds[0], 2, lambda i: (other, x))
    begin(sums)
    backward.send()

    d_gated = ref.inverse[...] * (
        ref.d_normed[...] * gain - ref.unit[...] * jnp.mean(ref.d_normed[...] * gain * ref.unit[...], axis=1, keepdims=True)
    )
    gate_grad[...] = (d_gated * ref.inner[...] * ref.slope[...]).astype(BF16)

    ref.a1[...] = ring_a.end_sum(ref.mine, left)
    ref.b1[...] = ring_b.end_sum(ref.mine, right)
    ref.a1_out[...] = ref.a1[...].astype(BF16)
    ref.b1_out[...] = ref.b1[...].astype(BF16)
    second = to_each(
        NY, ref.a2_s, ref.a2_r, along_y, lambda i: ref.a1_out.at[rows((y + i) % NY, 32)], lambda i: ref.a2.at[i - 1]
    ) + to_each(
        NX, ref.b2_s, ref.b2_r, along_x, lambda i: ref.b1_out.at[rows((x + i) % NX, 32)], lambda i: ref.b2.at[i - 1]
    )
    begin(second)
    backward.fold()
    rounds[1].mine[...] = sum_end(rounds[0], sums)
    sums = sum_round(rounds[1], NX, along_x)
    begin(sums)

    end(second)
    a2 = ref.a1[rows(y, 32), :] + (ref.a2[0].astype(F32) + ref.a2[1].astype(F32) + ref.a2[2].astype(F32))
    b2 = ref.b1[rows(x, 32), :] + (ref.b2[0].astype(F32) + ref.b2[1].astype(F32) + ref.b2[2].astype(F32))
    for k in range(4):
        part = (slice(16 * (k // 2), 16 * (k // 2) + 16), slice(256 * (k % 2), 256 * (k % 2) + 256))
        ref.c1[k] = a2[part]
        ref.c1[k + 4] = b2[part]
    third = to_each(
        NZ, ref.c3_s, ref.c3_r, along_z, lambda i: ref.c1.at[(z + i) % NZ], lambda i: ref.c3.at[i - 1]
    )
    begin(third)
    backward.answer()
    rounds[2].mine[...] = sum_end(rounds[1], sums)
    sums = sum_round(rounds[2], NY, along_y)
    begin(sums)
    pulled, pushed = ref.pulled[...], ref.pushed[...]
    paired = jnp.where(lower, mm_split(pulled, pushed, 1, 1), 0.0)
    ref.d_b[...] = mm_exact_right(paired, c, 0, 0)
    d_c = mm_exact_right(paired, b) + mm_split(pulled, ref.entering[...], 1, 1)
    pair_grad[:, STATE : 2 * STATE] = d_c.astype(BF16)

    end(third)
    block = ref.c1[pl.ds(z, 1)][0]
    for i in range(NZ - 1):
        block = block + ref.c3[i]
    ref.c4[pl.ds(z, 1)] = block.astype(BF16)[None]
    mine = ref.c4.at[z]
    fourth = to_each(NZ, ref.c4_s, ref.c4_r, along_z, lambda i: mine, lambda i: mine)
    begin(fourth)
    backward.halve()
    rounds[3].mine[...] = sum_end(rounds[2], sums)
    sums = sum_round(rounds[3], NZ, along_z)
    begin(sums)
    ref.d_x[...] = mm_split(ref.mixing[...], ref.pulled[...], 0, 0)

    end(fourth)
    base = core * 512
    for k in range(4):
        lanes = slice(256 * (k % 2), 256 * (k % 2) + 256)
        full[rows(k // 2, 16, base + 128 * x + 32 * y), lanes] = ref.c4[k]
        lanes = slice(512 + 256 * (k % 2), 512 + 256 * (k % 2) + 256)
        full[rows(k // 2, 16, base + 128 * y + 32 * x), lanes] = ref.c4[k + 4]
    at_a = full.at[rows(y, 32, base + 128 * x), left]
    at_b = full.at[rows(x, 32, base + 128 * y), right]
    fifth = to_each(NY, ref.a5_s, ref.a5_r, along_y, lambda i: at_a, lambda i: at_a) + to_each(
        NX, ref.b5_s, ref.b5_r, along_x, lambda i: at_b, lambda i: at_b
    )
    begin(fifth)
    backward.finish(ref.leaving, ref.half[0:1])
    end(fifth)
    ring_a.start_gather(full, base, left)
    ring_b.start_gather(full, base, right)

    last = []

    def hand_over(index, lanes):
        k, at = len(last), full.at[rows(index % 4, 128, base), lanes]
        last.append(copy_to(at, at, ref.last_s.at[k], ref.last_r.at[k], other, x))
        last[-1].start()

    hand_over(x, left)
    hand_over(y, right)
    leaving = ref.leaving[...]
    pair_grad[:, 0:STATE] = (ref.d_b[...] + mm_split(ref.pushed[...], leaving, 1, 1)).astype(BF16)
    ring_a.pass_gather()
    ring_b.pass_gather()
    input_grad[...] = (
        ref.down[...] * (ref.d_x[...] + mm_exact_left(b, leaving)) + ref.skip[0:1] * ref.d_mixed[...]
    ).astype(BF16)
    end([ring_a.gathers[2]])
    hand_over(x + 3, left)
    end([ring_b.gathers[2]])
    hand_over(y + 3, right)
    end([ring_a.gathers[3]])
    hand_over(x + 1, left)
    end([ring_b.gathers[3]])
    hand_over(y + 1, right)
    total[...] = sum_end(rounds[3], sums)
    end(ring_a.gathers[4:6])
    hand_over(x + 2, left)
    end(ring_b.gathers[4:6])
    hand_over(y + 2, right)
    end(last)


PARTS = 8


def widen(
    total, full_in, input_grad_in, gate_grad_in, pair_grad_in,
    full_out, gain, skip, input_grad_out, gate_grad_out, pair_grad_out,
    wide, saves, moves,
):
    moved = ((input_grad_in, input_grad_out), (gate_grad_in, gate_grad_out), (pair_grad_in, pair_grad_out))
    store = [pltpu.make_async_copy(src, dst, moves.at[k]) for k, (src, dst) in enumerate(moved)]
    begin(store)
    size = W // PARTS
    saved = []
    for k in range(PARTS):
        at = pl.ds(size * k, size)
        wide[at, :] = full_in[at, :].astype(F32)
        saved.append(pltpu.make_async_copy(wide.at[at], full_out.at[at], saves.at[k]))
        saved[k].start()
    for k in range(8):
        gain[0:1, 128 * k : 128 * k + 128] = total[k : k + 1]
    lane, head = iota((8, 128), 1), iota((8, HEADS), 1)
    first = jnp.sum(jnp.where(lane < 64, total[8:16], 0.0), axis=1, keepdims=True)
    second = jnp.sum(jnp.where(lane < 64, 0.0, total[8:16]), axis=1, keepdims=True)
    both = jnp.where(head % 2 == 0, first, second)
    skip[...] = jnp.sum(jnp.where(head // 2 == iota((8, HEADS), 0), both, 0.0), axis=0, keepdims=True)
    end(saved)
    end(store)


ANY = pl.BlockSpec(memory_space=pl.ANY)
VM = pl.BlockSpec(memory_space=pltpu.VMEM)
SM = pl.BlockSpec(memory_space=pltpu.SMEM)


def local(inputs, gates, pairs, steps, log_decay, skip, gain, out_weight, out_grad, order_ids):
    token, pair = ((T, W), BF16), ((T, 2 * STATE), BF16)
    input_grad, gate_grad, pair_grad, full, total = pl.pallas_call(
        kernel,
        out_shape=[pltpu.VMEM(*one) for one in (token, token, pair, ((W, W), BF16), ((16, 128), F32))],
        in_specs=[SM, VM, VM, VM] + [ANY] * 6,
        out_specs=[VM] * 5,
        scratch_shapes=[one for group in BUFFERS for one in group.values()],
        compiler_params=pltpu.CompilerParams(vmem_limit_bytes=VMEM_LIMIT, collective_id=0, has_side_effects=True),
    )(
        order_ids, log_decay[None], skip[None], gain[None], inputs[0], gates[0], pairs[0], steps[0], out_weight, out_grad[0]
    )

    weight_grad, gain_grad, skip_grad, input_grad, gate_grad, pair_grad = pl.pallas_call(
        widen,
        out_shape=[
            jax.ShapeDtypeStruct(*one) for one in (((W, W), F32), ((1, W), F32), ((1, HEADS), F32), token, token, pair)
        ],
        in_specs=[VM] * 5,
        out_specs=[ANY, VM, VM, ANY, ANY, ANY],
        scratch_shapes=[pltpu.VMEM((W, W), F32), dma(PARTS), dma(3)],
        compiler_params=pltpu.CompilerParams(vmem_limit_bytes=16 * 1024 * 1024),
    )(total, full, input_grad, gate_grad, pair_grad)
    return input_grad[None], gate_grad[None], pair_grad[None], weight_grad, gain_grad[0], skip_grad[0]


def solution(mesh):
    token = P("dp", "seq", None)
    return jax.shard_map(
        local,
        mesh=mesh,
        in_specs=(token, token, token, P("dp", None, "seq"), P(), P(), P(), P(), token, P()),
        out_specs=(token, token, token, P(), P(), P()),
        check_vma=False,
    )
```

```python
import types

import jax
import jax.numpy as jnp
from jax import lax
from jax.experimental import pallas as pl
from jax.experimental.pallas import tpu as pltpu
from jax.sharding import PartitionSpec as P

F32 = jnp.float32
BF16 = jnp.bfloat16
MESH = pl.DeviceIdType.MESH
EPSILON = 1e-05
T = 256
W = 1024
HEADS = 16
STATE = 64
SEQ, NX, NY, NZ, GROUP = 64, 4, 4, 8, 16
VMEM_LIMIT = 56 * 1024 * 1024


def iota(shape, dim):
    return lax.broadcasted_iota(jnp.int32, shape, dim)


def mm(a, b, ca=1, cb=0):
    return lax.dot_general(a, b, (((ca,), (cb,)), ((), ())), preferred_element_type=F32)


def split(a):
    high = a.astype(BF16)
    return high, (a - high.astype(F32)).astype(BF16)


def mm_exact_left(a, b, ca=1, cb=0):
    high, low = split(b)
    return mm(a, high, ca, cb) + mm(a, low, ca, cb)


def mm_exact_right(a, b, ca=1, cb=0):
    high, low = split(a)
    return mm(high, b, ca, cb) + mm(low, b, ca, cb)


def mm_split(a, b, ca=1, cb=0):
    ah, al = split(a)
    bh, bl = split(b)
    return mm(ah, bh, ca, cb) + (mm(ah, bl, ca, cb) + mm(al, bh, ca, cb))


def terms(a):
    high = a.astype(BF16)
    rest = a - high.astype(F32)
    mid = rest.astype(BF16)
    return high, mid, (rest - mid.astype(F32)).astype(BF16)


def expand(small):
    spread = (iota((HEADS, W), 1) // (W // HEADS) == iota((HEADS, W), 0)).astype(F32).astype(BF16)
    high, mid, low = terms(small)
    return mm(high, spread) + (mm(mid, spread) + mm(low, spread))


def scales(steps, log_decay):
    token_steps = steps.T
    lower = (iota((T, T), 0) >= iota((T, T), 1)).astype(F32).astype(BF16)
    high, mid, low = terms(token_steps * (-jnp.exp(log_decay)))
    logs = mm(lower, high) + (mm(lower, mid) + mm(lower, low))
    mid = 0.5 * logs[T - 1 : T, :]
    down = expand(jnp.exp(mid - logs) * token_steps)
    half = expand(jnp.broadcast_to(jnp.exp(mid), (8, HEADS)))
    return jnp.exp(logs - mid), down, half


def place():
    s = lax.axis_index("seq")
    return s, lax.axis_index("dp"), s // GROUP, s % GROUP


def copy_to(src, dst, send, recv, seq, dp):
    return pltpu.make_async_remote_copy(
        src_ref=src, dst_ref=dst, send_sem=send, recv_sem=recv, device_id={"seq": seq, "dp": dp}, device_id_type=MESH
    )


def each(count, act, start=1):
    def body(i, carry):
        act(i)
        return carry

    lax.fori_loop(start, count, body, 0)


def far_first(count):
    return sorted(range(1, count), key=lambda i: -min(i, count - i))


def begin(copies):
    for one in copies:
        one.start()


def end(copies):
    for one in copies:
        one.wait()


def rows(i, size, base=0):
    return pl.ds(pl.multiple_of(base + i * size, size), size)


def dma(*count):
    return pltpu.SemaphoreType.DMA(count)


class StateExchange:
    def __init__(self, ref, wire, reverse):
        self.ref, self.reverse, self.wire = ref, reverse, wire
        self.s, self.x, self.y, m = place()
        self.m, self.z, self.core = m, m // 2, m % 2
        self.other = self.s + 1 - 2 * self.core
        self.early = self.core == (1 if reverse else 0)

    @staticmethod
    def scratch(wire, back):
        tiles = 5 if wire == F32 else 6
        return dict(
            stage=pltpu.VMEM((2, NZ, 4, 8, 128), F32),
            decay=pltpu.VMEM((8, 128), F32),
            peer=pltpu.VMEM((NZ, 4, 8, 128), F32),
            peer_decay=pltpu.VMEM((8, 128), F32),
            out=pltpu.VMEM((NZ, 8 * tiles, 128), wire),
            inc=pltpu.VMEM((NZ, 8 * tiles, 128), wire),
            fold=pltpu.VMEM((NZ, tiles, 8, 128), F32),
            tot=pltpu.VMEM((5, 8, 128), F32),
            tots=pltpu.VMEM((NY, 5, 8, 128), F32),
            ans=pltpu.VMEM((NZ, 32, 128), back),
            got=pltpu.VMEM((NZ, 32, 128), back),
            give=pltpu.VMEM((NZ, 4, 8, 128), F32),
            take=pltpu.VMEM((NZ, 4, 8, 128), F32),
            s0=dma(3),
            r0=dma(3),
            s1=dma(NZ),
            r1=dma(NZ),
            s2=dma(NY),
            r2=dma(NY),
            s3=dma(NZ),
            r3=dma(NZ),
        )

    def pair(self, k):
        r = self.ref
        src, dst = ((r.stage.at[1 - self.core], r.peer), (r.decay, r.peer_decay), (r.give, r.take))[k]
        return copy_to(src, dst, r.s0.at[k], r.r0.at[k], self.other, self.x)

    def along_z(self, src, dst, send, recv, i):
        to = (self.z + i) % NZ
        return copy_to(
            src.at[to], dst.at[self.z], send.at[i], recv.at[i], self.y * GROUP + to * 2 + self.core, self.x
        )

    def first(self, i):
        return self.along_z(self.ref.out, self.ref.inc, self.ref.s1, self.ref.r1, i)

    def second(self, i):
        r, to = self.ref, (self.y + i) % NY
        return copy_to(r.tot, r.tots.at[self.y], r.s2.at[i], r.r2.at[i], to * GROUP + self.m, self.x)

    def third(self, i):
        return self.along_z(self.ref.ans, self.ref.got, self.ref.s3, self.ref.r3, i)

    def start(self, state, decay):
        r = self.ref
        for b in range(8):
            lanes = slice(128 * b, 128 * b + 128)
            r.decay[b : b + 1] = decay[0:1, lanes]
            for k in range(4):
                for core in range(2):
                    at = 16 * k + 8 * core
                    r.stage[core, :, k, b, :] = state[at : at + 8, lanes]

    def share(self):
        begin([self.pair(1), self.pair(0)])

    def send(self):
        r = self.ref
        end([self.pair(1), self.pair(0)])
        own, peer = r.stage[pl.ds(self.core, 1)][0], r.peer[...]
        mine, theirs = r.decay[...], r.peer_decay[...]
        early = jnp.full((8, 128), self.early.astype(jnp.int32)) > 0
        own_factor, peer_factor = jnp.where(early, theirs, 1.0), jnp.where(early, 1.0, mine)
        r.fold[:, 0:4] = own_factor * own + peer_factor * peer
        both = mine * theirs
        if self.wire == F32:
            r.fold[:, 4] = jnp.broadcast_to(both, (NZ, 8, 128))
        else:
            high = both.astype(BF16).astype(F32)
            r.fold[:, 4] = jnp.broadcast_to(high, (NZ, 8, 128))
            r.fold[:, 5] = jnp.broadcast_to(both - high, (NZ, 8, 128))
        r.out[...] = r.fold[...].reshape(r.out.shape).astype(self.wire)
        begin([self.first(i) for i in far_first(NZ)])
        r.inc[pl.ds(self.z, 1)] = r.out[pl.ds(self.z, 1)]

    def fold(self):
        r = self.ref
        end([self.first(i) for i in far_first(NZ)])
        r.fold[...] = r.inc[...].astype(F32).reshape(r.fold.shape)
        total, decay = jnp.zeros((4, 8, 128), F32), jnp.ones((8, 128), F32)
        for j in range(NZ)[:: -1 if self.reverse else 1]:
            block = r.fold[j]
            r.fold[j, 0:4] = total
            r.fold[j, 4] = decay
            factor = block[4] if self.wire == F32 else block[4] + block[5]
            total, decay = factor[None] * total + block[0:4], factor * decay
        r.tot[0:4] = total
        r.tot[4] = decay
        begin([self.second(i) for i in far_first(NY)])
        r.tots[pl.ds(self.y, 1)] = r.tot[...][None]

    def answer(self):
        r = self.ref
        end([self.second(i) for i in far_first(NY)])
        before = jnp.zeros((4, 8, 128), F32)
        for j in range(NY)[:: -1 if self.reverse else 1]:
            reached = (self.y < j) if self.reverse else (self.y > j)
            flag = jnp.full((4, 8, 128), reached.astype(jnp.int32)) > 0
            before = jnp.where(flag, r.tots[j, 4][None] * before + r.tots[j, 0:4], before)
        answers = r.fold[:, 0:4] + r.fold[:, 4:5] * before[None]
        r.ans[...] = answers.reshape(r.ans.shape).astype(r.ans.dtype)
        begin([self.third(i) for i in far_first(NZ)])
        r.got[pl.ds(self.z, 1)] = r.ans[pl.ds(self.z, 1)]

    def halve(self):
        r = self.ref
        end([self.third(i) for i in far_first(NZ)])
        entering = r.got[...].astype(F32).reshape(NZ, 4, 8, 128)
        own, peer = r.stage[pl.ds(self.core, 1)][0], r.peer[...]
        early = jnp.full((NZ, 4, 8, 128), self.early.astype(jnp.int32)) > 0
        r.give[...] = jnp.where(early, r.decay[...] * entering + own, entering)
        begin([self.pair(2)])
        r.stage[pl.ds(self.core, 1)] = jnp.where(early, entering, r.peer_decay[...] * entering + peer)[None]

    def finish(self, state_ref, scale):
        r = self.ref
        end([self.pair(2)])
        r.stage[pl.ds(1 - self.core, 1)] = r.take[...][None]
        for b in range(8):
            lanes = slice(128 * b, 128 * b + 128)
            for k in range(4):
                for core in range(2):
                    at = 16 * k + 8 * core
                    state_ref[at : at + 8, lanes] = r.stage[core, :, k, b, :] * scale[:, lanes]


class Ring:
    def __init__(self, ref, me, device):
        self.ref, self.me, self.right, self.left = ref, me, device(1), device(3)

    @staticmethod
    def scratch():
        half, whole = pltpu.VMEM((64, 512), BF16), pltpu.VMEM((128, 512), BF16)
        return dict(
            in_left=half, in_right=half, to_right=half, to_left=half, from_left=whole, from_right=whole,
            s1=dma(6), r1=dma(6), s6=dma(6), r6=dma(6),
        )

    def one(self, k, src, dst, device, send, recv):
        return copy_to(src, dst, send.at[k], recv.at[k], *device)

    def start_sum(self, rough, lanes):
        r, me = self.ref, self.me
        far, right, left = 128 * ((me + 2) % 4), 128 * ((me + 1) % 4), 128 * ((me + 3) % 4)
        top, low = slice(0, 64), slice(64, 128)
        parts = (
            (rough.at[rows(0, 64, far), lanes], r.in_left, self.right),
            (rough.at[rows(1, 64, far), lanes], r.in_right, self.left),
            (rough.at[rows(1, 64, right), lanes], r.from_left.at[low], self.right),
            (rough.at[rows(0, 64, left), lanes], r.from_right.at[top], self.left),
            (r.to_right, r.from_left.at[top], self.right),
            (r.to_left, r.from_right.at[low], self.left),
        )
        self.sums = [self.one(k, *part, r.s1, r.r1) for k, part in enumerate(parts)]
        begin(self.sums[0:4])

    def pass_sum(self, mine, lanes):
        r, me = self.ref, self.me
        end(self.sums[0:1])
        r.to_right[...] = (mine[rows(0, 64, 128 * ((me + 1) % 4)), lanes] + r.in_left[...].astype(F32)).astype(BF16)
        begin(self.sums[4:5])
        end(self.sums[1:2])
        r.to_left[...] = (mine[rows(1, 64, 128 * ((me + 3) % 4)), lanes] + r.in_right[...].astype(F32)).astype(BF16)
        begin(self.sums[5:6])

    def end_sum(self, mine, lanes):
        r = self.ref
        end(self.sums[2:6])
        return mine[rows(self.me, 128), lanes] + (r.from_left[...].astype(F32) + r.from_right[...].astype(F32))

    def start_gather(self, full, base, lanes):
        r, me = self.ref, self.me

        def half(j, low):
            return full.at[rows(low, 64, base + 128 * ((me + j) % 4)), lanes]

        def send(k, j, low, device):
            return self.one(k, half(j, low), half(j, low), device, r.s6, r.r6)

        self.gathers = [
            send(0, 0, 0, self.right),
            send(1, 0, 1, self.left),
            send(2, 0, 1, self.right),
            send(3, 0, 0, self.left),
            send(4, 3, 0, self.right),
            send(5, 1, 1, self.left),
        ]
        begin(self.gathers[0:4])

    def pass_gather(self):
        end(self.gathers[0:1])
        begin(self.gathers[4:5])
        end(self.gathers[1:2])
        begin(self.gathers[5:6])


def buffers():
    full, half = pltpu.VMEM((T, W), F32), pltpu.VMEM((T, W), BF16)
    out = dict(
        x=half,
        z=half,
        og=half,
        bc=pltpu.VMEM((T, 2 * STATE), BF16),
        dt=pltpu.VMEM((HEADS, T), F32),
        w=pltpu.VMEM((W, W), BF16),
        entered=pltpu.SemaphoreType.REGULAR,
        load=dma(6),
        swap_out=pltpu.VMEM((SEQ, 16, 256), BF16),
        swap_in=pltpu.VMEM((SEQ, 16, 256), BF16),
        swap_s=dma(SEQ),
        swap_r=dma(SEQ),
        grads=half,
        u=pltpu.VMEM((T, HEADS), F32),
        up=full,
        down=full,
        half=pltpu.VMEM((8, W), F32),
        skip=pltpu.VMEM((8, W), F32),
        pushed=full,
        mixing=pltpu.VMEM((T, T), F32),
        inner=full,
        active=full,
        slope=full,
        entering=pltpu.VMEM((STATE, W), F32),
        leaving=pltpu.VMEM((STATE, W), F32),
        inverse=pltpu.VMEM((T, 1), F32),
        unit=full,
        normed=half,
        d_normed=full,
        d_mixed=full,
        pulled=full,
        d_x=full,
        d_b=pltpu.VMEM((T, STATE), F32),
        peer_normed=pltpu.VMEM((T, 512), BF16),
        peer_grads=half,
        pair_s=dma(2),
        pair_r=dma(2),
        mine=pltpu.VMEM((512, W), F32),
        rough=pltpu.VMEM((512, W), BF16),
        a1=pltpu.VMEM((128, 512), F32),
        b1=pltpu.VMEM((128, 512), F32),
        a1_out=pltpu.VMEM((128, 512), BF16),
        b1_out=pltpu.VMEM((128, 512), BF16),
        a2=pltpu.VMEM((3, 32, 512), BF16),
        b2=pltpu.VMEM((3, 32, 512), BF16),
        a2_s=dma(4), a2_r=dma(4), b2_s=dma(4), b2_r=dma(4),
        c1=pltpu.VMEM((8, 16, 256), F32),
        c1_out=pltpu.VMEM((8, 16, 256), BF16),
        c3=pltpu.VMEM((7, 16, 256), BF16),
        c3_s=dma(8), c3_r=dma(8), c4_s=dma(8), c4_r=dma(8),
        c4=pltpu.VMEM((8, 16, 256), BF16),
        c5_s=dma(8, 4), c5_r=dma(8, 4),
        last_s=dma(8), last_r=dma(8),
    )
    rounds = [
        dict(
            mine=pltpu.VMEM((16, 128), F32), theirs=pltpu.VMEM((count - 1, 16, 128), F32), s=dma(count), r=dma(count)
        )
        for count in (2, NX, NY, NZ)
    ]
    return [out, StateExchange.scratch(*FORWARD), StateExchange.scratch(*BACKWARD), Ring.scratch(), Ring.scratch(), *rounds]


FORWARD, BACKWARD = (F32, F32), (F32, F32)
BUFFERS = buffers()


def kernel(
    orders, decay_ref, skip_ref, gain_ref, x_in, z_in, bc_in, dt_in, w_in, og_in,
    input_grad, gate_grad, pair_grad, full, total, *scratch,
):
    scratch = iter(scratch)
    ref, ref_f, ref_b, ring_a, ring_b, *rounds = [
        types.SimpleNamespace(**{key: next(scratch) for key in group}) for group in BUFFERS
    ]
    s, x, y, m = place()
    z, core = m // 2, m % 2
    other = s + 1 - 2 * core

    barrier = pltpu.get_barrier_semaphore()

    def hello(seq, dp):
        pl.semaphore_signal(barrier, inc=1, device_id=dict(seq=seq, dp=dp), device_id_type=MESH)

    operands = ((dt_in, ref.dt), (bc_in, ref.bc), (x_in, ref.x), (og_in, ref.og), (z_in, ref.z), (w_in, ref.w))
    loads = [pltpu.make_async_copy(src, dst, ref.load.at[k]) for k, (src, dst) in enumerate(operands)]
    begin(loads)
    for i in far_first(GROUP):
        hello(y * GROUP + (m + i) % GROUP, x)
    for i in far_first(NY):
        hello(((y + i) % NY) * GROUP + m, x)
    for i in far_first(NX):
        hello(s, (x + i) % NX)

    end(loads[0:1])
    ref.u[...], down, half = scales(ref.dt[...], decay_ref[...])
    ref.down[...], ref.half[...] = down, half
    end(loads[1:3])
    ref.pushed[...] = down * ref.x[...].astype(F32)
    forward = StateExchange(ref_f, FORWARD[0], False)
    b, c = ref.bc[:, 0:STATE], ref.bc[:, STATE : 2 * STATE]
    forward.start(half[0:1] * mm_exact_left(b, ref.pushed[...], 0, 0), half * half)
    pl.semaphore_wait(barrier, GROUP - 1 + NY - 1 + NX - 1)
    for i in far_first(NY):
        pl.semaphore_signal(
            ref.entered, inc=1, device_id=dict(seq=((y + i) % NY) * GROUP + m, dp=x), device_id_type=MESH
        )
    forward.share()

    forward.send()

    flip_rows = (orders[0] + orders[1]) % 2
    flip_columns = (orders[0] // 2 + orders[1] // 2 + s) % 2
    row = iota((4 * T, T), 0)
    device, quarter, line = row // 16, (row // 4) % 4, row % 4
    token = line * SEQ + jnp.where((line + flip_rows) % 2 == 0, device, SEQ - 1 - device)
    column = iota((4 * T, T), 1)
    end(loads[3:4])
    packed = jnp.zeros((4 * T, T), F32)
    for j in range(4):
        pick = jnp.where((token == column) & (quarter == j), 1.0, 0.0).astype(BF16)
        packed = packed + mm(pick, ref.og[:, 256 * j : 256 * j + 256])
    ref.swap_out[...] = packed.astype(BF16).reshape(SEQ, 16, 256)

    pl.semaphore_wait(ref.entered, NY - 1)

    def swap(i):
        to = (s + i) % SEQ
        return copy_to(ref.swap_out.at[to], ref.swap_in.at[s], ref.swap_s.at[i], ref.swap_r.at[i], to, x)

    each(SEQ, lambda i: swap(i).start())
    ref.swap_in[pl.ds(s, 1)] = ref.swap_out[pl.ds(s, 1)]

    lower = iota((T, T), 0) >= iota((T, T), 1)
    ref.mixing[...] = jnp.where(lower, mm(c, b, 1, 1), 0.0)
    ref.inner[...] = mm_split(ref.mixing[...], ref.pushed[...])
    ref.up[...] = expand(ref.u[...])
    ref.skip[...] = expand(jnp.broadcast_to(skip_ref[...], (8, HEADS)))
    forward.fold()
    end(loads[4:5])
    gate = ref.z[...].astype(F32)
    sigma = jax.nn.sigmoid(gate)
    ref.active[...] = gate * sigma
    ref.slope[...] = sigma * (1.0 + gate * (1.0 - sigma))
    forward.answer()
    forward.halve()

    each(SEQ, lambda i: swap(i).wait())
    arrived = ref.swap_in[...].reshape(4 * T, 256)
    at = iota((T, 4 * T), 0)
    source = jnp.where(flip_columns == 0, at, T - 1 - at)
    source = (source // 4) * 16 + source % 4
    column = iota((T, 4 * T), 1)
    for j in range(4):
        pick = jnp.where(source + 4 * j == column, 1.0, 0.0).astype(BF16)
        ref.grads[:, 256 * j : 256 * j + 256] = mm(pick, arrived).astype(BF16)
    share_grads = copy_to(ref.grads, ref.peer_grads, ref.pair_s.at[0], ref.pair_r.at[0], other, x)
    share_grads.start()

    forward.finish(ref.entering, ref.half[0:1])
    gain = gain_ref[...]
    mixed = ref.up[...] * (ref.inner[...] + mm_exact_left(c, ref.entering[...]))
    mixed = mixed + ref.skip[0:1] * ref.x[...].astype(F32)
    ref.inner[...] = mixed
    gated = mixed * ref.active[...]
    inverse = lax.rsqrt(jnp.mean(gated * gated, axis=1, keepdims=True) + EPSILON)
    ref.inverse[...] = inverse
    unit = gated * inverse
    ref.unit[...] = unit
    ref.normed[...] = (unit * gain).astype(BF16)

    share_normed = copy_to(
        ref.normed.at[:, rows(1 - core, 512)], ref.peer_normed, ref.pair_s.at[1], ref.pair_r.at[1], other, x
    )
    share_normed.start()
    ref.mine[...] = mm(ref.normed[:, rows(core, 512)], ref.grads[...], 0, 0)
    end([share_grads, share_normed])
    ref.mine[...] += mm(ref.peer_normed[...], ref.peer_grads[...], 0, 0)
    ref.rough[...] = ref.mine[...].astype(BF16)

    def along_x(i):
        return s, (x + i) % NX

    def along_y(i):
        return ((y + i) % NY) * GROUP + m, x

    def along_z(i):
        return y * GROUP + ((z + i) % NZ) * 2 + core, x

    def to_each(count, send, recv, peer, src, dst):
        return [copy_to(src(i), dst(i), send.at[i], recv.at[i], *peer(i)) for i in far_first(count)]

    left, right = slice(0, 512), slice(512, 1024)
    ring_a, ring_b = Ring(ring_a, x, along_x), Ring(ring_b, y, along_y)
    ring_a.start_sum(ref.rough, left)
    ring_b.start_sum(ref.rough, right)

    end(loads[5:6])
    d_normed = mm(ref.grads[...], ref.w[...], 1, 1)
    ref.d_normed[...] = d_normed
    unit = ref.unit[...]
    scaled = d_normed * gain
    d_gated = ref.inverse[...] * (scaled - unit * jnp.mean(scaled * unit, axis=1, keepdims=True))
    d_mixed = d_gated * ref.active[...]
    ref.d_mixed[...] = d_mixed
    ref.pulled[...] = ref.up[...] * d_mixed
    backward = StateExchange(ref_b, BACKWARD[0], True)
    half = ref.half[...]
    backward.start(half[0:1] * mm_exact_left(c, ref.pulled[...], 0, 0), half * half)
    backward.share()
    ring_a.pass_sum(ref.mine, left)
    ring_b.pass_sum(ref.mine, right)
    gain_sum = jnp.sum(ref.d_normed[...] * ref.unit[...], axis=0, keepdims=True)
    skip_sum = jnp.sum(ref.d_mixed[...] * ref.x[...].astype(F32), axis=0, keepdims=True)
    for k in range(8):
        lanes = slice(128 * k, 128 * k + 128)
        rounds[0].mine[k : k + 1] = gain_sum[:, lanes]
        rounds[0].mine[8 + k : 9 + k] = skip_sum[:, lanes]

    def sum_round(one, count, peer):
        return to_each(count, one.s, one.r, peer, lambda i: one.mine, lambda i: one.theirs.at[i - 1])

    def sum_end(one, copies):
        end(copies)
        total = one.mine[...]
        for i in range(len(copies)):
            total = total + one.theirs[i]
        return total

    sums = sum_round(rounds[0], 2, lambda i: (other, x))
    begin(sums)
    backward.send()

    d_gated = ref.inverse[...] * (
        ref.d_normed[...] * gain - ref.unit[...] * jnp.mean(ref.d_normed[...] * gain * ref.unit[...], axis=1, keepdims=True)
    )
    gate_grad[...] = (d_gated * ref.inner[...] * ref.slope[...]).astype(BF16)

    ref.a1[...] = ring_a.end_sum(ref.mine, left)
    ref.b1[...] = ring_b.end_sum(ref.mine, right)
    ref.a1_out[...] = ref.a1[...].astype(BF16)
    ref.b1_out[...] = ref.b1[...].astype(BF16)
    second = to_each(
        NY, ref.a2_s, ref.a2_r, along_y, lambda i: ref.a1_out.at[rows((y + i) % NY, 32)], lambda i: ref.a2.at[i - 1]
    ) + to_each(
        NX, ref.b2_s, ref.b2_r, along_x, lambda i: ref.b1_out.at[rows((x + i) % NX, 32)], lambda i: ref.b2.at[i - 1]
    )
    begin(second)
    backward.fold()
    rounds[1].mine[...] = sum_end(rounds[0], sums)
    sums = sum_round(rounds[1], NX, along_x)
    begin(sums)

    end(second)
    a2 = ref.a1[rows(y, 32), :] + (ref.a2[0].astype(F32) + ref.a2[1].astype(F32) + ref.a2[2].astype(F32))
    b2 = ref.b1[rows(x, 32), :] + (ref.b2[0].astype(F32) + ref.b2[1].astype(F32) + ref.b2[2].astype(F32))
    for k in range(4):
        part = (slice(16 * (k // 2), 16 * (k // 2) + 16), slice(256 * (k % 2), 256 * (k % 2) + 256))
        ref.c1[k] = a2[part]
        ref.c1[k + 4] = b2[part]
    ref.c1_out[...] = ref.c1[...].astype(BF16)
    third = to_each(
        NZ, ref.c3_s, ref.c3_r, along_z, lambda i: ref.c1_out.at[(z + i) % NZ], lambda i: ref.c3.at[i - 1]
    )
    begin(third)
    backward.answer()
    rounds[2].mine[...] = sum_end(rounds[1], sums)
    sums = sum_round(rounds[2], NY, along_y)
    begin(sums)
    pulled, pushed = ref.pulled[...], ref.pushed[...]
    paired = jnp.where(lower, mm_split(pulled, pushed, 1, 1), 0.0)
    ref.d_b[...] = mm_exact_right(paired, c, 0, 0)
    d_c = mm_exact_right(paired, b) + mm_split(pulled, ref.entering[...], 1, 1)
    pair_grad[:, STATE : 2 * STATE] = d_c.astype(BF16)

    end(third)
    block = ref.c1[pl.ds(z, 1)][0]
    for i in range(NZ - 1):
        block = block + ref.c3[i].astype(F32)
    ref.c4[pl.ds(z, 1)] = block.astype(BF16)[None]
    mine = ref.c4.at[z]
    fourth = dict(zip(far_first(NZ), to_each(NZ, ref.c4_s, ref.c4_r, along_z, lambda i: mine, lambda i: mine)))
    begin(fourth.values())

    base, fifth = core * 512, []

    def spread(j):
        over_x = j // 4
        outer, inner = x + over_x * (y - x), y + over_x * (x - y)
        at = (
            rows((j % 4) // 2, 16, base + 128 * outer + 32 * inner),
            pl.ds(pl.multiple_of(512 * over_x + 256 * (j % 2), 256), 256),
        )
        for i in far_first(NX):
            seq = s + (1 - over_x) * (((y + i) % NY) * GROUP + m - s)
            dp = x + over_x * ((x + i) % NX - x)
            fifth.append(copy_to(ref.c4.at[j], full.at[at], ref.c5_s.at[j, i], ref.c5_r.at[j, i], seq, dp))
            fifth[-1].start()
        full[at] = ref.c4[pl.ds(j, 1)][0]

    spread(z)
    backward.halve()
    rounds[3].mine[...] = sum_end(rounds[2], sums)
    sums = sum_round(rounds[3], NZ, along_z)
    begin(sums)
    for i in far_first(NZ)[::-1]:
        fourth[i].wait()
        spread((z + NZ - i) % NZ)
    ref.d_x[...] = mm_split(ref.mixing[...], ref.pulled[...], 0, 0)
    backward.finish(ref.leaving, ref.half[0:1])
    leaving = ref.leaving[...]
    input_grad[...] = (
        ref.down[...] * (ref.d_x[...] + mm_exact_left(b, leaving)) + ref.skip[0:1] * ref.d_mixed[...]
    ).astype(BF16)
    end(fifth)
    ring_a.start_gather(full, base, left)
    ring_b.start_gather(full, base, right)

    last = []

    def hand_over(index, lanes):
        k, at = len(last), full.at[rows(index % 4, 128, base), lanes]
        last.append(copy_to(at, at, ref.last_s.at[k], ref.last_r.at[k], other, x))
        last[-1].start()

    hand_over(x, left)
    hand_over(y, right)
    ring_a.pass_gather()
    ring_b.pass_gather()
    end([ring_a.gathers[2]])
    hand_over(x + 3, left)
    end([ring_b.gathers[2]])
    hand_over(y + 3, right)
    end([ring_a.gathers[3]])
    hand_over(x + 1, left)
    end([ring_b.gathers[3]])
    hand_over(y + 1, right)
    total[...] = sum_end(rounds[3], sums)
    pair_grad[:, 0:STATE] = (ref.d_b[...] + mm_split(ref.pushed[...], leaving, 1, 1)).astype(BF16)
    end(ring_a.gathers[4:6])
    hand_over(x + 2, left)
    end(ring_b.gathers[4:6])
    hand_over(y + 2, right)
    end(last)


PARTS = 8


def widen(
    total, full_in, input_grad_in, gate_grad_in, pair_grad_in,
    full_out, gain, skip, input_grad_out, gate_grad_out, pair_grad_out,
    wide, saves, moves,
):
    moved = ((input_grad_in, input_grad_out), (gate_grad_in, gate_grad_out), (pair_grad_in, pair_grad_out))
    store = [pltpu.make_async_copy(src, dst, moves.at[k]) for k, (src, dst) in enumerate(moved)]
    begin(store)
    size = W // PARTS
    saved = []
    for k in range(PARTS):
        at = pl.ds(size * k, size)
        wide[at, :] = full_in[at, :].astype(F32)
        saved.append(pltpu.make_async_copy(wide.at[at], full_out.at[at], saves.at[k]))
        saved[k].start()
    for k in range(8):
        gain[0:1, 128 * k : 128 * k + 128] = total[k : k + 1]
    lane, head = iota((8, 128), 1), iota((8, HEADS), 1)
    first = jnp.sum(jnp.where(lane < 64, total[8:16], 0.0), axis=1, keepdims=True)
    second = jnp.sum(jnp.where(lane < 64, 0.0, total[8:16]), axis=1, keepdims=True)
    both = jnp.where(head % 2 == 0, first, second)
    skip[...] = jnp.sum(jnp.where(head // 2 == iota((8, HEADS), 0), both, 0.0), axis=0, keepdims=True)
    end(saved)
    end(store)


ANY = pl.BlockSpec(memory_space=pl.ANY)
VM = pl.BlockSpec(memory_space=pltpu.VMEM)
SM = pl.BlockSpec(memory_space=pltpu.SMEM)


def local(inputs, gates, pairs, steps, log_decay, skip, gain, out_weight, out_grad, order_ids):
    token, pair = ((T, W), BF16), ((T, 2 * STATE), BF16)
    input_grad, gate_grad, pair_grad, full, total = pl.pallas_call(
        kernel,
        out_shape=[pltpu.VMEM(*one) for one in (token, token, pair, ((W, W), BF16), ((16, 128), F32))],
        in_specs=[SM, VM, VM, VM] + [ANY] * 6,
        out_specs=[VM] * 5,
        scratch_shapes=[one for group in BUFFERS for one in group.values()],
        compiler_params=pltpu.CompilerParams(vmem_limit_bytes=VMEM_LIMIT, collective_id=0, has_side_effects=True),
    )(
        order_ids, log_decay[None], skip[None], gain[None], inputs[0], gates[0], pairs[0], steps[0], out_weight, out_grad[0]
    )

    weight_grad, gain_grad, skip_grad, input_grad, gate_grad, pair_grad = pl.pallas_call(
        widen,
        out_shape=[
            jax.ShapeDtypeStruct(*one) for one in (((W, W), F32), ((1, W), F32), ((1, HEADS), F32), token, token, pair)
        ],
        in_specs=[VM] * 5,
        out_specs=[ANY, VM, VM, ANY, ANY, ANY],
        scratch_shapes=[pltpu.VMEM((W, W), F32), dma(PARTS), dma(3)],
        compiler_params=pltpu.CompilerParams(vmem_limit_bytes=16 * 1024 * 1024),
    )(total, full, input_grad, gate_grad, pair_grad)
    return input_grad[None], gate_grad[None], pair_grad[None], weight_grad, gain_grad[0], skip_grad[0]


def solution(mesh):
    token = P("dp", "seq", None)
    return jax.shard_map(
        local,
        mesh=mesh,
        in_specs=(token, token, token, P("dp", None, "seq"), P(), P(), P(), P(), token, P()),
        out_specs=(token, token, token, P(), P(), P()),
        check_vma=False,
    )
```

```python
import types

import jax
import jax.numpy as jnp
from jax import lax
from jax.experimental import pallas as pl
from jax.experimental.pallas import tpu as pltpu
from jax.sharding import PartitionSpec as P

F32 = jnp.float32
BF16 = jnp.bfloat16
MESH = pl.DeviceIdType.MESH
EPSILON = 1e-05
T = 256
W = 1024
HEADS = 16
STATE = 64
SEQ, NX, NY, NZ, GROUP = 64, 4, 4, 8, 16
VMEM_LIMIT = 56 * 1024 * 1024


def iota(shape, dim):
    return lax.broadcasted_iota(jnp.int32, shape, dim)


def mm(a, b, ca=1, cb=0):
    return lax.dot_general(a, b, (((ca,), (cb,)), ((), ())), preferred_element_type=F32)


def split(a):
    high = a.astype(BF16)
    return high, (a - high.astype(F32)).astype(BF16)


def mm_exact_left(a, b, ca=1, cb=0):
    high, low = split(b)
    return mm(a, high, ca, cb) + mm(a, low, ca, cb)


def mm_exact_right(a, b, ca=1, cb=0):
    high, low = split(a)
    return mm(high, b, ca, cb) + mm(low, b, ca, cb)


def mm_split(a, b, ca=1, cb=0):
    ah, al = split(a)
    bh, bl = split(b)
    return mm(ah, bh, ca, cb) + (mm(ah, bl, ca, cb) + mm(al, bh, ca, cb))


def terms(a):
    high = a.astype(BF16)
    rest = a - high.astype(F32)
    mid = rest.astype(BF16)
    return high, mid, (rest - mid.astype(F32)).astype(BF16)


def expand(small):
    spread = (iota((HEADS, W), 1) // (W // HEADS) == iota((HEADS, W), 0)).astype(F32).astype(BF16)
    high, mid, low = terms(small)
    return mm(high, spread) + (mm(mid, spread) + mm(low, spread))


def scales(steps, log_decay):
    token_steps = steps.T
    lower = (iota((T, T), 0) >= iota((T, T), 1)).astype(F32).astype(BF16)
    high, mid, low = terms(token_steps * (-jnp.exp(log_decay)))
    logs = mm(lower, high) + (mm(lower, mid) + mm(lower, low))
    mid = 0.5 * logs[T - 1 : T, :]
    down = expand(jnp.exp(mid - logs) * token_steps)
    half = expand(jnp.broadcast_to(jnp.exp(mid), (8, HEADS)))
    return jnp.exp(logs - mid), down, half


def place():
    s = lax.axis_index("seq")
    return s, lax.axis_index("dp"), s // GROUP, s % GROUP


def copy_to(src, dst, send, recv, seq, dp):
    return pltpu.make_async_remote_copy(
        src_ref=src, dst_ref=dst, send_sem=send, recv_sem=recv, device_id={"seq": seq, "dp": dp}, device_id_type=MESH
    )


def each(count, act, start=1):
    def body(i, carry):
        act(i)
        return carry

    lax.fori_loop(start, count, body, 0)


def far_first(count):
    return sorted(range(1, count), key=lambda i: -min(i, count - i))


def begin(copies):
    for one in copies:
        one.start()


def end(copies):
    for one in copies:
        one.wait()


def rows(i, size, base=0):
    return pl.ds(pl.multiple_of(base + i * size, size), size)


def dma(*count):
    return pltpu.SemaphoreType.DMA(count)


class StateExchange:
    def __init__(self, ref, wire, reverse):
        self.ref, self.reverse, self.wire = ref, reverse, wire
        self.s, self.x, self.y, m = place()
        self.m, self.z, self.core = m, m // 2, m % 2
        self.other = self.s + 1 - 2 * self.core
        self.early = self.core == (1 if reverse else 0)

    @staticmethod
    def scratch(wire, back):
        tiles = 5 if wire == F32 else 6
        return dict(
            stage=pltpu.VMEM((2, NZ, 4, 8, 128), F32),
            decay=pltpu.VMEM((8, 128), F32),
            peer=pltpu.VMEM((NZ, 4, 8, 128), F32),
            peer_decay=pltpu.VMEM((8, 128), F32),
            out=pltpu.VMEM((NZ, 8 * tiles, 128), wire),
            inc=pltpu.VMEM((NZ, 8 * tiles, 128), wire),
            fold=pltpu.VMEM((NZ, tiles, 8, 128), F32),
            tot=pltpu.VMEM((5, 8, 128), F32),
            tots=pltpu.VMEM((NY, 5, 8, 128), F32),
            ans=pltpu.VMEM((NZ, 32, 128), back),
            got=pltpu.VMEM((NZ, 32, 128), back),
            give=pltpu.VMEM((NZ, 4, 8, 128), F32),
            take=pltpu.VMEM((NZ, 4, 8, 128), F32),
            s0=dma(3),
            r0=dma(3),
            s1=dma(NZ),
            r1=dma(NZ),
            s2=dma(NY),
            r2=dma(NY),
            s3=dma(NZ),
            r3=dma(NZ),
        )

    def pair(self, k):
        r = self.ref
        src, dst = ((r.stage.at[1 - self.core], r.peer), (r.decay, r.peer_decay), (r.give, r.take))[k]
        return copy_to(src, dst, r.s0.at[k], r.r0.at[k], self.other, self.x)

    def along_z(self, src, dst, send, recv, i):
        to = (self.z + i) % NZ
        return copy_to(
            src.at[to], dst.at[self.z], send.at[i], recv.at[i], self.y * GROUP + to * 2 + self.core, self.x
        )

    def first(self, i):
        return self.along_z(self.ref.out, self.ref.inc, self.ref.s1, self.ref.r1, i)

    def second(self, i):
        r, to = self.ref, (self.y + i) % NY
        return copy_to(r.tot, r.tots.at[self.y], r.s2.at[i], r.r2.at[i], to * GROUP + self.m, self.x)

    def third(self, i):
        return self.along_z(self.ref.ans, self.ref.got, self.ref.s3, self.ref.r3, i)

    def start(self, state, decay):
        r = self.ref
        for b in range(8):
            lanes = slice(128 * b, 128 * b + 128)
            r.decay[b : b + 1] = decay[0:1, lanes]
            for k in range(4):
                for core in range(2):
                    at = 16 * k + 8 * core
                    r.stage[core, :, k, b, :] = state[at : at + 8, lanes]

    def share(self):
        begin([self.pair(1), self.pair(0)])

    def send(self):
        r = self.ref
        end([self.pair(1), self.pair(0)])
        own, peer = r.stage[pl.ds(self.core, 1)][0], r.peer[...]
        mine, theirs = r.decay[...], r.peer_decay[...]
        early = jnp.full((8, 128), self.early.astype(jnp.int32)) > 0
        own_factor, peer_factor = jnp.where(early, theirs, 1.0), jnp.where(early, 1.0, mine)
        r.fold[:, 0:4] = own_factor * own + peer_factor * peer
        both = mine * theirs
        if self.wire == F32:
            r.fold[:, 4] = jnp.broadcast_to(both, (NZ, 8, 128))
        else:
            high = both.astype(BF16).astype(F32)
            r.fold[:, 4] = jnp.broadcast_to(high, (NZ, 8, 128))
            r.fold[:, 5] = jnp.broadcast_to(both - high, (NZ, 8, 128))
        r.out[...] = r.fold[...].reshape(r.out.shape).astype(self.wire)
        begin([self.first(i) for i in far_first(NZ)])
        r.inc[pl.ds(self.z, 1)] = r.out[pl.ds(self.z, 1)]

    def fold(self):
        r = self.ref
        end([self.first(i) for i in far_first(NZ)])
        r.fold[...] = r.inc[...].astype(F32).reshape(r.fold.shape)
        total, decay = jnp.zeros((4, 8, 128), F32), jnp.ones((8, 128), F32)
        for j in range(NZ)[:: -1 if self.reverse else 1]:
            block = r.fold[j]
            r.fold[j, 0:4] = total
            r.fold[j, 4] = decay
            factor = block[4] if self.wire == F32 else block[4] + block[5]
            total, decay = factor[None] * total + block[0:4], factor * decay
        r.tot[0:4] = total
        r.tot[4] = decay
        begin([self.second(i) for i in far_first(NY)])
        r.tots[pl.ds(self.y, 1)] = r.tot[...][None]

    def answer(self):
        r = self.ref
        end([self.second(i) for i in far_first(NY)])
        before = jnp.zeros((4, 8, 128), F32)
        for j in range(NY)[:: -1 if self.reverse else 1]:
            reached = (self.y < j) if self.reverse else (self.y > j)
            flag = jnp.full((4, 8, 128), reached.astype(jnp.int32)) > 0
            before = jnp.where(flag, r.tots[j, 4][None] * before + r.tots[j, 0:4], before)
        answers = r.fold[:, 0:4] + r.fold[:, 4:5] * before[None]
        r.ans[...] = answers.reshape(r.ans.shape).astype(r.ans.dtype)
        begin([self.third(i) for i in far_first(NZ)])
        r.got[pl.ds(self.z, 1)] = r.ans[pl.ds(self.z, 1)]

    def halve(self):
        r = self.ref
        end([self.third(i) for i in far_first(NZ)])
        entering = r.got[...].astype(F32).reshape(NZ, 4, 8, 128)
        own, peer = r.stage[pl.ds(self.core, 1)][0], r.peer[...]
        early = jnp.full((NZ, 4, 8, 128), self.early.astype(jnp.int32)) > 0
        r.give[...] = jnp.where(early, r.decay[...] * entering + own, entering)
        begin([self.pair(2)])
        r.stage[pl.ds(self.core, 1)] = jnp.where(early, entering, r.peer_decay[...] * entering + peer)[None]

    def finish(self, state_ref, scale):
        r = self.ref
        end([self.pair(2)])
        r.stage[pl.ds(1 - self.core, 1)] = r.take[...][None]
        for b in range(8):
            lanes = slice(128 * b, 128 * b + 128)
            for k in range(4):
                for core in range(2):
                    at = 16 * k + 8 * core
                    state_ref[at : at + 8, lanes] = r.stage[core, :, k, b, :] * scale[:, lanes]


class Ring:
    def __init__(self, ref, me, device):
        self.ref, self.me, self.right, self.left = ref, me, device(1), device(3)

    @staticmethod
    def scratch():
        half, whole = pltpu.VMEM((64, 512), BF16), pltpu.VMEM((128, 512), BF16)
        return dict(
            in_left=half, in_right=half, to_right=half, to_left=half, from_left=whole, from_right=whole,
            s1=dma(6), r1=dma(6), s6=dma(6), r6=dma(6),
        )

    def one(self, k, src, dst, device, send, recv):
        return copy_to(src, dst, send.at[k], recv.at[k], *device)

    def start_sum(self, rough, lanes):
        r, me = self.ref, self.me
        far, right, left = 128 * ((me + 2) % 4), 128 * ((me + 1) % 4), 128 * ((me + 3) % 4)
        top, low = slice(0, 64), slice(64, 128)
        parts = (
            (rough.at[rows(0, 64, far), lanes], r.in_left, self.right),
            (rough.at[rows(1, 64, far), lanes], r.in_right, self.left),
            (rough.at[rows(1, 64, right), lanes], r.from_left.at[low], self.right),
            (rough.at[rows(0, 64, left), lanes], r.from_right.at[top], self.left),
            (r.to_right, r.from_left.at[top], self.right),
            (r.to_left, r.from_right.at[low], self.left),
        )
        self.sums = [self.one(k, *part, r.s1, r.r1) for k, part in enumerate(parts)]
        begin(self.sums[0:4])

    def pass_sum(self, mine, lanes):
        r, me = self.ref, self.me
        end(self.sums[0:1])
        r.to_right[...] = (mine[rows(0, 64, 128 * ((me + 1) % 4)), lanes] + r.in_left[...].astype(F32)).astype(BF16)
        begin(self.sums[4:5])
        end(self.sums[1:2])
        r.to_left[...] = (mine[rows(1, 64, 128 * ((me + 3) % 4)), lanes] + r.in_right[...].astype(F32)).astype(BF16)
        begin(self.sums[5:6])

    def end_sum(self, mine, lanes):
        r = self.ref
        end(self.sums[2:6])
        return mine[rows(self.me, 128), lanes] + (r.from_left[...].astype(F32) + r.from_right[...].astype(F32))

    def start_gather(self, full, base, lanes):
        r, me = self.ref, self.me

        def half(j, low):
            return full.at[rows(low, 64, base + 128 * ((me + j) % 4)), lanes]

        def send(k, j, low, device):
            return self.one(k, half(j, low), half(j, low), device, r.s6, r.r6)

        self.gathers = [
            send(0, 0, 0, self.right),
            send(1, 0, 1, self.left),
            send(2, 0, 1, self.right),
            send(3, 0, 0, self.left),
            send(4, 3, 0, self.right),
            send(5, 1, 1, self.left),
        ]
        begin(self.gathers[0:4])

    def pass_gather(self):
        end(self.gathers[0:1])
        begin(self.gathers[4:5])
        end(self.gathers[1:2])
        begin(self.gathers[5:6])


def buffers():
    full, half = pltpu.VMEM((T, W), F32), pltpu.VMEM((T, W), BF16)
    out = dict(
        x=half,
        z=half,
        og=half,
        bc=pltpu.VMEM((T, 2 * STATE), BF16),
        dt=pltpu.VMEM((HEADS, T), F32),
        w=pltpu.VMEM((W, W), BF16),
        entered=pltpu.SemaphoreType.REGULAR,
        load=dma(6),
        swap_out=pltpu.VMEM((SEQ, 16, 256), BF16),
        swap_in=pltpu.VMEM((SEQ, 16, 256), BF16),
        swap_s=dma(SEQ),
        swap_r=dma(SEQ),
        grads=half,
        u=pltpu.VMEM((T, HEADS), F32),
        up=full,
        down=full,
        half=pltpu.VMEM((8, W), F32),
        skip=pltpu.VMEM((8, W), F32),
        pushed=full,
        mixing=pltpu.VMEM((T, T), F32),
        inner=full,
        active=full,
        slope=full,
        entering=pltpu.VMEM((STATE, W), F32),
        leaving=pltpu.VMEM((STATE, W), F32),
        inverse=pltpu.VMEM((T, 1), F32),
        unit=full,
        normed=half,
        d_normed=full,
        d_mixed=full,
        pulled=full,
        d_x=full,
        d_b=pltpu.VMEM((T, STATE), F32),
        peer_normed=pltpu.VMEM((T, 512), BF16),
        peer_grads=half,
        pair_s=dma(2),
        pair_r=dma(2),
        mine=pltpu.VMEM((512, W), F32),
        rough=pltpu.VMEM((512, W), BF16),
        a1=pltpu.VMEM((128, 512), F32),
        b1=pltpu.VMEM((128, 512), F32),
        a1_out=pltpu.VMEM((128, 512), BF16),
        b1_out=pltpu.VMEM((128, 512), BF16),
        a2=pltpu.VMEM((3, 32, 512), BF16),
        b2=pltpu.VMEM((3, 32, 512), BF16),
        a2_s=dma(4), a2_r=dma(4), b2_s=dma(4), b2_r=dma(4),
        c1=pltpu.VMEM((8, 16, 256), F32),
        c1_out=pltpu.VMEM((8, 16, 256), BF16),
        c3=pltpu.VMEM((7, 16, 256), BF16),
        c3_s=dma(8), c3_r=dma(8), c4_s=dma(8), c4_r=dma(8),
        c4=pltpu.VMEM((8, 16, 256), BF16),
        c5_s=dma(8, 4), c5_r=dma(8, 4),
        last_s=dma(8), last_r=dma(8),
    )
    rounds = [
        dict(
            mine=pltpu.VMEM((16, 128), F32), theirs=pltpu.VMEM((count - 1, 16, 128), F32), s=dma(count), r=dma(count)
        )
        for count in (2, NX, NY, NZ)
    ]
    return [out, StateExchange.scratch(*FORWARD), StateExchange.scratch(*BACKWARD), Ring.scratch(), Ring.scratch(), *rounds]


FORWARD, BACKWARD = (F32, F32), (F32, F32)
BUFFERS = buffers()


def kernel(
    orders, decay_ref, skip_ref, gain_ref, x_in, z_in, bc_in, dt_in, w_in, og_in,
    input_grad, gate_grad, pair_grad, full, total, *scratch,
):
    scratch = iter(scratch)
    ref, ref_f, ref_b, ring_a, ring_b, *rounds = [
        types.SimpleNamespace(**{key: next(scratch) for key in group}) for group in BUFFERS
    ]
    s, x, y, m = place()
    z, core = m // 2, m % 2
    other = s + 1 - 2 * core

    barrier = pltpu.get_barrier_semaphore()

    def hello(seq, dp):
        pl.semaphore_signal(barrier, inc=1, device_id=dict(seq=seq, dp=dp), device_id_type=MESH)

    operands = ((dt_in, ref.dt), (bc_in, ref.bc), (x_in, ref.x), (og_in, ref.og), (z_in, ref.z), (w_in, ref.w))
    loads = [pltpu.make_async_copy(src, dst, ref.load.at[k]) for k, (src, dst) in enumerate(operands)]
    begin(loads)
    for i in far_first(GROUP):
        hello(y * GROUP + (m + i) % GROUP, x)
    for i in far_first(NY):
        hello(((y + i) % NY) * GROUP + m, x)
    for i in far_first(NX):
        hello(s, (x + i) % NX)

    end(loads[0:1])
    ref.u[...], down, half = scales(ref.dt[...], decay_ref[...])
    ref.down[...], ref.half[...] = down, half
    end(loads[1:3])
    ref.pushed[...] = down * ref.x[...].astype(F32)
    forward = StateExchange(ref_f, FORWARD[0], False)
    b, c = ref.bc[:, 0:STATE], ref.bc[:, STATE : 2 * STATE]
    forward.start(half[0:1] * mm_exact_left(b, ref.pushed[...], 0, 0), half * half)
    pl.semaphore_wait(barrier, GROUP - 1 + NY - 1 + NX - 1)
    for i in far_first(NY):
        pl.semaphore_signal(
            ref.entered, inc=1, device_id=dict(seq=((y + i) % NY) * GROUP + m, dp=x), device_id_type=MESH
        )
    forward.share()

    forward.send()

    flip_rows = (orders[0] + orders[1]) % 2
    flip_columns = (orders[0] // 2 + orders[1] // 2 + s) % 2
    row = iota((4 * T, T), 0)
    device, quarter, line = row // 16, (row // 4) % 4, row % 4
    token = line * SEQ + jnp.where((line + flip_rows) % 2 == 0, device, SEQ - 1 - device)
    column = iota((4 * T, T), 1)
    end(loads[3:4])
    packed = jnp.zeros((4 * T, T), F32)
    for j in range(4):
        pick = jnp.where((token == column) & (quarter == j), 1.0, 0.0).astype(BF16)
        packed = packed + mm(pick, ref.og[:, 256 * j : 256 * j + 256])
    ref.swap_out[...] = packed.astype(BF16).reshape(SEQ, 16, 256)

    pl.semaphore_wait(ref.entered, NY - 1)

    def swap(i):
        to = (s + i) % SEQ
        return copy_to(ref.swap_out.at[to], ref.swap_in.at[s], ref.swap_s.at[i], ref.swap_r.at[i], to, x)

    each(SEQ, lambda i: swap(i).start())
    ref.swap_in[pl.ds(s, 1)] = ref.swap_out[pl.ds(s, 1)]

    lower = iota((T, T), 0) >= iota((T, T), 1)
    ref.mixing[...] = jnp.where(lower, mm(c, b, 1, 1), 0.0)
    ref.inner[...] = mm_split(ref.mixing[...], ref.pushed[...])
    ref.up[...] = expand(ref.u[...])
    ref.skip[...] = expand(jnp.broadcast_to(skip_ref[...], (8, HEADS)))
    forward.fold()
    end(loads[4:5])
    gate = ref.z[...].astype(F32)
    sigma = jax.nn.sigmoid(gate)
    ref.active[...] = gate * sigma
    ref.slope[...] = sigma * (1.0 + gate * (1.0 - sigma))
    forward.answer()
    forward.halve()

    each(SEQ, lambda i: swap(i).wait())
    arrived = ref.swap_in[...].reshape(4 * T, 256)
    at = iota((T, 4 * T), 0)
    source = jnp.where(flip_columns == 0, at, T - 1 - at)
    source = (source // 4) * 16 + source % 4
    column = iota((T, 4 * T), 1)
    for j in range(4):
        pick = jnp.where(source + 4 * j == column, 1.0, 0.0).astype(BF16)
        ref.grads[:, 256 * j : 256 * j + 256] = mm(pick, arrived).astype(BF16)
    share_grads = copy_to(ref.grads, ref.peer_grads, ref.pair_s.at[0], ref.pair_r.at[0], other, x)
    share_grads.start()

    forward.finish(ref.entering, ref.half[0:1])
    gain = gain_ref[...]
    mixed = ref.up[...] * (ref.inner[...] + mm_exact_left(c, ref.entering[...]))
    mixed = mixed + ref.skip[0:1] * ref.x[...].astype(F32)
    ref.inner[...] = mixed
    gated = mixed * ref.active[...]
    inverse = lax.rsqrt(jnp.mean(gated * gated, axis=1, keepdims=True) + EPSILON)
    ref.inverse[...] = inverse
    unit = gated * inverse
    ref.unit[...] = unit
    ref.normed[...] = (unit * gain).astype(BF16)

    share_normed = copy_to(
        ref.normed.at[:, rows(1 - core, 512)], ref.peer_normed, ref.pair_s.at[1], ref.pair_r.at[1], other, x
    )
    share_normed.start()
    ref.mine[...] = mm(ref.normed[:, rows(core, 512)], ref.grads[...], 0, 0)
    end([share_grads, share_normed])
    ref.mine[...] += mm(ref.peer_normed[...], ref.peer_grads[...], 0, 0)
    ref.rough[...] = ref.mine[...].astype(BF16)

    def along_x(i):
        return s, (x + i) % NX

    def along_y(i):
        return ((y + i) % NY) * GROUP + m, x

    def along_z(i):
        return y * GROUP + ((z + i) % NZ) * 2 + core, x

    def to_each(count, send, recv, peer, src, dst):
        return [copy_to(src(i), dst(i), send.at[i], recv.at[i], *peer(i)) for i in far_first(count)]

    left, right = slice(0, 512), slice(512, 1024)
    ring_a, ring_b = Ring(ring_a, x, along_x), Ring(ring_b, y, along_y)
    ring_a.start_sum(ref.rough, left)
    ring_b.start_sum(ref.rough, right)

    end(loads[5:6])
    d_normed = mm(ref.grads[...], ref.w[...], 1, 1)
    ref.d_normed[...] = d_normed
    unit = ref.unit[...]
    scaled = d_normed * gain
    d_gated = ref.inverse[...] * (scaled - unit * jnp.mean(scaled * unit, axis=1, keepdims=True))
    d_mixed = d_gated * ref.active[...]
    ref.d_mixed[...] = d_mixed
    ref.pulled[...] = ref.up[...] * d_mixed
    backward = StateExchange(ref_b, BACKWARD[0], True)
    half = ref.half[...]
    backward.start(half[0:1] * mm_exact_left(c, ref.pulled[...], 0, 0), half * half)
    backward.share()
    ring_a.pass_sum(ref.mine, left)
    ring_b.pass_sum(ref.mine, right)
    gain_sum = jnp.sum(ref.d_normed[...] * ref.unit[...], axis=0, keepdims=True)
    skip_sum = jnp.sum(ref.d_mixed[...] * ref.x[...].astype(F32), axis=0, keepdims=True)
    for k in range(8):
        lanes = slice(128 * k, 128 * k + 128)
        rounds[0].mine[k : k + 1] = gain_sum[:, lanes]
        rounds[0].mine[8 + k : 9 + k] = skip_sum[:, lanes]

    def sum_round(one, count, peer):
        return to_each(count, one.s, one.r, peer, lambda i: one.mine, lambda i: one.theirs.at[i - 1])

    def sum_end(one, copies):
        end(copies)
        total = one.mine[...]
        for i in range(len(copies)):
            total = total + one.theirs[i]
        return total

    sums = sum_round(rounds[0], 2, lambda i: (other, x))
    begin(sums)
    backward.send()

    d_gated = ref.inverse[...] * (
        ref.d_normed[...] * gain - ref.unit[...] * jnp.mean(ref.d_normed[...] * gain * ref.unit[...], axis=1, keepdims=True)
    )
    gate_grad[...] = (d_gated * ref.inner[...] * ref.slope[...]).astype(BF16)

    ref.a1[...] = ring_a.end_sum(ref.mine, left)
    ref.b1[...] = ring_b.end_sum(ref.mine, right)
    ref.a1_out[...] = ref.a1[...].astype(BF16)
    ref.b1_out[...] = ref.b1[...].astype(BF16)
    second = to_each(
        NY, ref.a2_s, ref.a2_r, along_y, lambda i: ref.a1_out.at[rows((y + i) % NY, 32)], lambda i: ref.a2.at[i - 1]
    ) + to_each(
        NX, ref.b2_s, ref.b2_r, along_x, lambda i: ref.b1_out.at[rows((x + i) % NX, 32)], lambda i: ref.b2.at[i - 1]
    )
    begin(second)
    backward.fold()
    rounds[1].mine[...] = sum_end(rounds[0], sums)
    sums = sum_round(rounds[1], NX, along_x)
    begin(sums)

    end(second)
    a2 = ref.a1[rows(y, 32), :] + (ref.a2[0].astype(F32) + ref.a2[1].astype(F32) + ref.a2[2].astype(F32))
    b2 = ref.b1[rows(x, 32), :] + (ref.b2[0].astype(F32) + ref.b2[1].astype(F32) + ref.b2[2].astype(F32))
    for k in range(4):
        part = (slice(16 * (k // 2), 16 * (k // 2) + 16), slice(256 * (k % 2), 256 * (k % 2) + 256))
        ref.c1[k] = a2[part]
        ref.c1[k + 4] = b2[part]
    ref.c1_out[...] = ref.c1[...].astype(BF16)
    third = to_each(
        NZ, ref.c3_s, ref.c3_r, along_z, lambda i: ref.c1_out.at[(z + i) % NZ], lambda i: ref.c3.at[i - 1]
    )
    begin(third)
    backward.answer()
    rounds[2].mine[...] = sum_end(rounds[1], sums)
    sums = sum_round(rounds[2], NY, along_y)
    begin(sums)
    pulled, pushed = ref.pulled[...], ref.pushed[...]
    paired = jnp.where(lower, mm_split(pulled, pushed, 1, 1), 0.0)
    ref.d_b[...] = mm_exact_right(paired, c, 0, 0)
    d_c = mm_exact_right(paired, b) + mm_split(pulled, ref.entering[...], 1, 1)
    pair_grad[:, STATE : 2 * STATE] = d_c.astype(BF16)

    end(third)
    block = ref.c1[pl.ds(z, 1)][0]
    for i in range(NZ - 1):
        block = block + ref.c3[i].astype(F32)
    ref.c4[pl.ds(z, 1)] = block.astype(BF16)[None]
    mine = ref.c4.at[z]
    fourth = dict(zip(far_first(NZ), to_each(NZ, ref.c4_s, ref.c4_r, along_z, lambda i: mine, lambda i: mine)))
    begin(fourth.values())

    base, fifth = core * 512, []

    def spread(j):
        over_x = j // 4
        outer, inner = x + over_x * (y - x), y + over_x * (x - y)
        at = (
            rows((j % 4) // 2, 16, base + 128 * outer + 32 * inner),
            pl.ds(pl.multiple_of(512 * over_x + 256 * (j % 2), 256), 256),
        )
        for i in far_first(NX):
            seq = s + (1 - over_x) * (((y + i) % NY) * GROUP + m - s)
            dp = x + over_x * ((x + i) % NX - x)
            fifth.append(copy_to(ref.c4.at[j], full.at[at], ref.c5_s.at[j, i], ref.c5_r.at[j, i], seq, dp))
            fifth[-1].start()
        full[at] = ref.c4[pl.ds(j, 1)][0]

    spread(z)
    ref.d_x[...] = mm_split(ref.mixing[...], ref.pulled[...], 0, 0)
    for i in far_first(NZ)[::-1]:
        fourth[i].wait()
        spread((z + NZ - i) % NZ)
    backward.halve()
    rounds[3].mine[...] = sum_end(rounds[2], sums)
    sums = sum_round(rounds[3], NZ, along_z)
    begin(sums)
    backward.finish(ref.leaving, ref.half[0:1])
    leaving = ref.leaving[...]
    input_grad[...] = (
        ref.down[...] * (ref.d_x[...] + mm_exact_left(b, leaving)) + ref.skip[0:1] * ref.d_mixed[...]
    ).astype(BF16)
    end(fifth)
    ring_a.start_gather(full, base, left)
    ring_b.start_gather(full, base, right)

    last = []

    def hand_over(index, lanes):
        k, at = len(last), full.at[rows(index % 4, 128, base), lanes]
        last.append(copy_to(at, at, ref.last_s.at[k], ref.last_r.at[k], other, x))
        last[-1].start()

    hand_over(x, left)
    hand_over(y, right)
    ring_a.pass_gather()
    ring_b.pass_gather()
    end([ring_a.gathers[2]])
    hand_over(x + 3, left)
    end([ring_b.gathers[2]])
    hand_over(y + 3, right)
    end([ring_a.gathers[3]])
    hand_over(x + 1, left)
    end([ring_b.gathers[3]])
    hand_over(y + 1, right)
    total[...] = sum_end(rounds[3], sums)
    pair_grad[:, 0:STATE] = (ref.d_b[...] + mm_split(ref.pushed[...], leaving, 1, 1)).astype(BF16)
    end(ring_a.gathers[4:6])
    hand_over(x + 2, left)
    end(ring_b.gathers[4:6])
    hand_over(y + 2, right)
    end(last)


PARTS = 8


def widen(
    total, full_in, input_grad_in, gate_grad_in, pair_grad_in,
    full_out, gain, skip, input_grad_out, gate_grad_out, pair_grad_out,
    wide, saves, moves,
):
    moved = ((input_grad_in, input_grad_out), (gate_grad_in, gate_grad_out), (pair_grad_in, pair_grad_out))
    store = [pltpu.make_async_copy(src, dst, moves.at[k]) for k, (src, dst) in enumerate(moved)]
    begin(store)
    size = W // PARTS
    saved = []
    for k in range(PARTS):
        at = pl.ds(size * k, size)
        wide[at, :] = full_in[at, :].astype(F32)
        saved.append(pltpu.make_async_copy(wide.at[at], full_out.at[at], saves.at[k]))
        saved[k].start()
    for k in range(8):
        gain[0:1, 128 * k : 128 * k + 128] = total[k : k + 1]
    lane, head = iota((8, 128), 1), iota((8, HEADS), 1)
    first = jnp.sum(jnp.where(lane < 64, total[8:16], 0.0), axis=1, keepdims=True)
    second = jnp.sum(jnp.where(lane < 64, 0.0, total[8:16]), axis=1, keepdims=True)
    both = jnp.where(head % 2 == 0, first, second)
    skip[...] = jnp.sum(jnp.where(head // 2 == iota((8, HEADS), 0), both, 0.0), axis=0, keepdims=True)
    end(saved)
    end(store)


ANY = pl.BlockSpec(memory_space=pl.ANY)
VM = pl.BlockSpec(memory_space=pltpu.VMEM)
SM = pl.BlockSpec(memory_space=pltpu.SMEM)


def local(inputs, gates, pairs, steps, log_decay, skip, gain, out_weight, out_grad, order_ids):
    token, pair = ((T, W), BF16), ((T, 2 * STATE), BF16)
    input_grad, gate_grad, pair_grad, full, total = pl.pallas_call(
        kernel,
        out_shape=[pltpu.VMEM(*one) for one in (token, token, pair, ((W, W), BF16), ((16, 128), F32))],
        in_specs=[SM, VM, VM, VM] + [ANY] * 6,
        out_specs=[VM] * 5,
        scratch_shapes=[one for group in BUFFERS for one in group.values()],
        compiler_params=pltpu.CompilerParams(vmem_limit_bytes=VMEM_LIMIT, collective_id=0, has_side_effects=True),
    )(
        order_ids, log_decay[None], skip[None], gain[None], inputs[0], gates[0], pairs[0], steps[0], out_weight, out_grad[0]
    )

    weight_grad, gain_grad, skip_grad, input_grad, gate_grad, pair_grad = pl.pallas_call(
        widen,
        out_shape=[
            jax.ShapeDtypeStruct(*one) for one in (((W, W), F32), ((1, W), F32), ((1, HEADS), F32), token, token, pair)
        ],
        in_specs=[VM] * 5,
        out_specs=[ANY, VM, VM, ANY, ANY, ANY],
        scratch_shapes=[pltpu.VMEM((W, W), F32), dma(PARTS), dma(3)],
        compiler_params=pltpu.CompilerParams(vmem_limit_bytes=16 * 1024 * 1024),
    )(total, full, input_grad, gate_grad, pair_grad)
    return input_grad[None], gate_grad[None], pair_grad[None], weight_grad, gain_grad[0], skip_grad[0]


def solution(mesh):
    token = P("dp", "seq", None)
    return jax.shard_map(
        local,
        mesh=mesh,
        in_specs=(token, token, token, P("dp", None, "seq"), P(), P(), P(), P(), token, P()),
        out_specs=(token, token, token, P(), P(), P()),
        check_vma=False,
    )
```
